128 devices in a mesh: section: 8 (over y, z_lo), fsdp: 16 (over x, z_hi, core).
Axes of the slice: x: 4, y: 4, z: 4 (z_hi: 2, z_lo: 2; z = z_hi * 2 + z_lo), core: 2. Of those that a mesh axis runs over, the one named last changes fastest.
Arguments:
- section_inputs: bfloat16 [8, 2, 2048, 8192], P('section', None, 'fsdp'), may hold values from -6 to 6
- top_grads: bfloat16 [2, 2048, 8192], P(None, 'fsdp'), may hold values from -6 to 6
- weights: bfloat16 [8, 8192, 512], P('section', 'fsdp'), may hold values from -0.125 to 0.125
- norm_gains: float32 [8, 8192], P('section', 'fsdp'), may hold values from 0.25 to 1.75
- feedback: float32 [8, 2048, 8192], P('section', 'fsdp'), may hold values from -4 to 4
- rotation_bits: int32 [8, 8192], replicated, may hold values from 0 to 1
- batch_order: int32 [2], replicated, may hold values from 0 to 1, each once
Outputs:
- input_grads: float32 [8, 2, 2048, 8192], P('section', None, 'fsdp')
- weight_grads: float32 [8, 8192, 512], P('section', 'fsdp')
- gain_grads: float32 [8, 8192], P('section', 'fsdp')
- feedback_out: float32 [8, 2048, 8192], P('section', 'fsdp')
The draws below stay inside these ranges and needn't reach their ends.
Inputs may be any that keep to these rules, and one draw needn't show every extreme that they name: `batch_order`: a permutation of the micro-batches.
All inputs are finite; a program needn't handle non-finite values.
Results may differ from the reference program's by a relative error of at most 0.035.
Values may be sent and summed in bfloat16 or wider, within the bound.
No kernel may reach another device: no remote copies, remote signals or barrier semaphores. Data moves between devices by JAX's collectives and lax.ppermute only.
A program may use at most 192 MiB of HBM per device.

```python
import jax
import jax.numpy as jnp
from jax import lax

D = 8192
R = 512
HB = 256
MB = 2
TOKENS = 2048
N_SECTION = 8


def set_ends(result, stream_key, low, top_value):
    spot = [jax.random.randint(jax.random.fold_in(stream_key, axis), (), 0, length) for axis, length in enumerate(result.shape)]
    longest = result.shape.index(max(result.shape))
    neighbour = spot[:longest] + [(spot[longest] + 1) % result.shape[longest]] + spot[longest + 1:]
    return result.at[tuple(spot)].set(low).at[tuple(neighbour)].set(top_value)


def block_levels(stream_key, dims, shards, smallest, top_value):
    level = 1.0
    for dim, shards_of in shards:
        draws = jax.random.uniform(jax.random.fold_in(jax.random.fold_in(stream_key, 6), dim), (shards_of,), jnp.float32, smallest / len(shards), top_value / len(shards))
        level = level * jnp.repeat(jnp.exp(draws), dims[dim] // shards_of).reshape((-1,) + (1,) * (len(dims) - 1 - dim))
    return level


def normal_values(own_key, shape, scale, reach, shards=(), kind=jnp.bfloat16):
    array = scale * jax.random.normal(own_key, shape, jnp.float32)
    if shards:
        array = array * block_levels(own_key, shape, shards, -0.22, 0.18)
    return jnp.clip(array, -reach, reach).astype(kind)


def setup_inputs(seed: int = 0) -> dict:
    splits = jax.random.split(jax.random.key(seed), 8)
    section_inputs = normal_values(splits[0], (N_SECTION, MB, TOKENS, D), 1.0, 6.0, ((0, 8), (2, 16)))
    top_grads = normal_values(splits[1], (MB, TOKENS, D), 1.0, 6.0, ((1, 16),))
    weights = normal_values(splits[2], (N_SECTION, D, R), (D // 4) ** -0.5, 0.125, ((0, 8), (1, 16)))
    norm_gains = jnp.clip(1.0 + 0.15 * jax.random.normal(splits[3], (N_SECTION, D), jnp.float32), 0.25, 1.75)
    feedback = normal_values(splits[4], (N_SECTION, TOKENS, D), 0.5, 4.0, ((0, 8), (1, 16)), jnp.float32)
    rotation_bits = set_ends(jax.random.randint(splits[5], (N_SECTION, D), 0, 2), jax.random.fold_in(splits[5], 1), 0, 1).astype(jnp.int32)
    batch_order = jax.random.permutation(splits[6], MB).astype(jnp.int32)
    return dict(section_inputs=section_inputs, top_grads=top_grads, weights=weights, norm_gains=norm_gains, feedback=feedback, rotation_bits=rotation_bits, batch_order=batch_order)


eps_norm = 1e-05
eps_scale = 1e-06
highest = lax.Precision.HIGHEST

def hadamard(order_size):
    position = jnp.arange(order_size, dtype=jnp.int32)
    shared_bits = jnp.bitwise_and(position[:, None], position[None, :])
    parity = jnp.zeros((order_size, order_size), jnp.int32)
    for bit_place in range(order_size.bit_length() - 1):
        parity = parity + jnp.bitwise_and(jnp.right_shift(shared_bits, bit_place), 1)
    return (1 - 2 * (parity % 2)).astype(jnp.float32) / jnp.sqrt(jnp.float32(order_size))

def rotate(values, sign_row, matrix):
    block_size = matrix.shape[0]
    blocks = (values * sign_row).reshape(values.shape[0], values.shape[1] // block_size, block_size)
    return jnp.einsum('tbk,kj->tbj', blocks, matrix, precision=highest)

def restore(rotated, sign_row, matrix):
    unrotated = jnp.einsum('tbk,kj->tbj', rotated, matrix, precision=highest)
    return unrotated.reshape(unrotated.shape[0], -1) * sign_row

def layer_backward(inputs, grad_in, gain_row, weight):
    values = inputs.astype(jnp.float32)
    scale_inv = lax.rsqrt(lax.optimization_barrier(jnp.mean(values * values, axis=-1, keepdims=True)) + eps_norm)
    normed = values * scale_inv
    hidden_in = (normed * gain_row).astype(jnp.bfloat16)
    grad_low = grad_in.astype(jnp.bfloat16)
    pre = jnp.dot(hidden_in, weight, preferred_element_type=jnp.float32)
    grad_act = jnp.dot(grad_low, weight, preferred_element_type=jnp.float32)
    sigma = jax.nn.sigmoid(pre)
    active_out = (pre * sigma).astype(jnp.bfloat16)
    grad_pre = (grad_act * sigma * (1.0 + pre * (1.0 - sigma))).astype(jnp.bfloat16)
    grad_hidden = lax.dot_general(grad_pre, weight, (((1,), (1,)), ((), ())), preferred_element_type=jnp.float32)
    gain_term = lax.optimization_barrier(jnp.sum(grad_hidden * normed, axis=0))
    grad_normed = grad_hidden * gain_row
    grad_out = grad_in + scale_inv * (grad_normed - normed * lax.optimization_barrier(jnp.mean(grad_normed * normed, axis=-1, keepdims=True)))
    return (grad_out, gain_term, hidden_in, grad_low, grad_pre, active_out)

def encode(grad_out, carried, sign_row, matrix):
    total = grad_out + carried
    rotated = rotate(total, sign_row, matrix)
    scale_low = (lax.optimization_barrier(jnp.mean(jnp.abs(rotated), axis=-1)) + eps_scale).astype(jnp.bfloat16)
    scale_wide = scale_low.astype(jnp.float32)[..., None]
    levels = jnp.clip(rotated / scale_wide, -1.0, 1.0).astype(jnp.bfloat16)
    decoded = restore(levels.astype(jnp.float32) * scale_wide, sign_row, matrix)
    return (total - decoded, decoded)

def reference(section_inputs, top_grads, weights, norm_gains, feedback, rotation_bits, batch_order):
    matrix = hadamard(HB)
    sign_rows = (1 - 2 * rotation_bits).astype(jnp.float32)
    adapter = weights.shape[2]
    carried = [feedback[section] for section in range(N_SECTION)]
    kept_hidden = [jnp.zeros((MB, TOKENS, D), jnp.bfloat16) for section in range(N_SECTION)]
    kept_grad = [jnp.zeros((MB, TOKENS, D), jnp.bfloat16) for section in range(N_SECTION)]
    kept_pre = [jnp.zeros((MB, TOKENS, adapter), jnp.bfloat16) for section in range(N_SECTION)]
    kept_act = [jnp.zeros((MB, TOKENS, adapter), jnp.bfloat16) for section in range(N_SECTION)]
    grads_kept = [jnp.zeros((MB, TOKENS, D), jnp.float32) for section in range(N_SECTION)]
    gain_sums = [jnp.zeros((D,), jnp.float32) for section in range(N_SECTION)]
    for slot in range(MB):
        micro = batch_order[slot]
        grad_in = top_grads[micro].astype(jnp.float32)
        for section in reversed(range(N_SECTION)):
            inputs = section_inputs[section][micro]
            grad_out, gain_term, hidden_in, grad_low, grad_pre, active_out = layer_backward(inputs, grad_in, norm_gains[section], weights[section])
            kept_hidden[section] = kept_hidden[section].at[micro].set(hidden_in)
            kept_grad[section] = kept_grad[section].at[micro].set(grad_low)
            kept_pre[section] = kept_pre[section].at[micro].set(grad_pre)
            kept_act[section] = kept_act[section].at[micro].set(active_out)
            grads_kept[section] = grads_kept[section].at[micro].set(grad_out)
            gain_sums[section] = gain_sums[section] + gain_term
            if section > 0:
                carried[section], grad_in = encode(grad_out, carried[section], sign_rows[section], matrix)
    weight_list = []
    for section in range(N_SECTION):
        left_rows = jnp.concatenate([kept_hidden[section].reshape(-1, D), kept_grad[section].reshape(-1, D)], axis=0)
        right_rows = jnp.concatenate([kept_pre[section].reshape(-1, adapter), kept_act[section].reshape(-1, adapter)], axis=0)
        summed = lax.dot_general(left_rows, right_rows, (((0,), (0,)), ((), ())), preferred_element_type=jnp.float32)
        weight_list.append(summed)
    input_grads = jnp.stack(grads_kept, axis=0)
    weight_grads = jnp.stack(weight_list, axis=0)
    gain_grads = jnp.stack(gain_sums, axis=0)
    feedback_out = jnp.stack(carried, axis=0)
    return (input_grads, weight_grads, gain_grads, feedback_out)
```

```python
import itertools

import jax
import jax.numpy as jnp
from jax import lax
from jax.experimental import pallas as pl
from jax.experimental.pallas import tpu as pltpu
from jax.sharding import Mesh
from jax.sharding import PartitionSpec as P

HB = 256
C = 32
eps_norm = 1e-05
eps_scale = 1e-06

AXES = ("y", "zl", "x", "zh", "core")
SIZES = (4, 2, 4, 2, 2)
SECTION = ("y", "zl")
FSDP = ("x", "zh", "core")
GROUP = ("x", "zh", "zl")
PAD = 16


def linear(y, zl, x, zh, core):
    return (((y * 2 + zl) * 4 + x) * 2 + zh) * 2 + core


def all_coords():
    return itertools.product(*(range(size) for size in SIZES))


def hop_pairs():
    pairs = []
    for y, zl, x, zh, core in all_coords():
        if core == 0:
            pairs.append((linear(y, zl, x, zh, 0), linear(y, zl, x, zh, 1)))
        elif y > 0:
            pairs.append((linear(y, zl, x, zh, 1), linear(y - 1, zl, x, zh, 0)))
    return pairs


def swap_pairs():
    pairs = []
    for y, zl, x, zh, core in all_coords():
        here = linear(y, zl, x, zh, core)
        pairs.append((here, linear(y, 1 - zl, x, zh, 1 - core) if zl == core else here))
    return pairs


def top_pairs():
    pairs = []
    for y, zl, x, zh, core in all_coords():
        if y == 3 and zl == 0 and core == 1:
            pairs.append((linear(y, zl, x, zh, 1), linear(y, zl, x, zh, 0)))
        elif y == 3 and zl == 1 and core == 0:
            pairs.append((linear(y, zl, x, zh, 0), linear(y, zl, x, zh, 0)))
    return pairs


def permuted(value, pairs):
    return lax.ppermute(value, AXES, pairs)


def hadamard(order_size):
    position = jnp.arange(order_size, dtype=jnp.int32)
    shared_bits = jnp.bitwise_and(position[:, None], position[None, :])
    parity = jnp.zeros((order_size, order_size), jnp.int32)
    for bit_place in range(order_size.bit_length() - 1):
        parity = parity + jnp.bitwise_and(jnp.right_shift(shared_bits, bit_place), 1)
    return ((1 - 2 * (parity % 2)).astype(jnp.float32) / 16.0).astype(jnp.bfloat16)


def dot(left, right):
    return jnp.dot(left, right, preferred_element_type=jnp.float32)


ANY = pl.BlockSpec(memory_space=pl.ANY)
VM = pl.BlockSpec(memory_space=pltpu.VMEM)
SM = pl.BlockSpec(memory_space=pltpu.SMEM)


def forward_kernel(w_hbm, x_ref, gain_ref, act_ref, slope_ref, inv_ref, w_ref, sems):
    shards = w_hbm.shape[0]
    rows = w_ref.shape[0] // shards

    def load(i):
        return pltpu.make_async_copy(
            w_hbm.at[i ^ 1, pl.ds(0, rows)], w_ref.at[pl.ds(i * rows, rows)], sems.at[i]
        )

    first = pl.program_id(0) == 0

    @pl.when(first)
    def _():
        for i in range(shards):
            load(i).start()

    width = x_ref.shape[1]
    total = None
    for i in range(width // 1024):
        part = x_ref[:, i * 1024 : (i + 1) * 1024].astype(jnp.float32)
        square = jnp.sum(part * part, axis=1, keepdims=True)
        total = square if total is None else total + square
    inv = lax.rsqrt(total / width + eps_norm)
    inv_ref[...] = jnp.broadcast_to(inv, inv_ref.shape)

    @pl.when(first)
    def _():
        for i in range(shards):
            load(i).wait()

    pre = None
    for i in range(shards):
        cols = slice(i * rows, (i + 1) * rows)
        hidden = (x_ref[:, cols].astype(jnp.float32) * inv * gain_ref[:, cols]).astype(jnp.bfloat16)
        part = dot(hidden, w_ref[cols, :])
        pre = part if pre is None else pre + part
    sigma = 1.0 / (1.0 + jnp.exp(-pre))
    act_ref[...] = (pre * sigma).astype(jnp.bfloat16)
    slope_ref[...] = sigma * (1.0 + pre * (1.0 - sigma))


def forward(weight, inputs, gain):
    tokens, width = inputs.shape
    adapter = weight.shape[2]
    block = 128
    return pl.pallas_call(
        forward_kernel,
        grid=(tokens // block,),
        in_specs=[
            ANY,
            pl.BlockSpec((block, width), lambda i: (i, 0)),
            pl.BlockSpec((1, width), lambda i: (0, 0)),
        ],
        out_specs=[
            pl.BlockSpec((block, adapter), lambda i: (i, 0)),
            pl.BlockSpec((block, adapter), lambda i: (i, 0)),
            pl.BlockSpec((block, 128), lambda i: (i, 0)),
        ],
        out_shape=[
            jax.ShapeDtypeStruct((tokens, adapter), jnp.bfloat16),
            jax.ShapeDtypeStruct((tokens, adapter), jnp.float32),
            jax.ShapeDtypeStruct((tokens, 128), jnp.float32),
        ],
        scratch_shapes=[
            pltpu.VMEM((width, adapter), jnp.bfloat16),
            pltpu.SemaphoreType.DMA((weight.shape[0],)),
        ],
        compiler_params=pltpu.CompilerParams(vmem_limit_bytes=32 * 1024 * 1024),
        name="forward_part",
    )(weight, inputs, gain)


def stage_kernel(
    s_ref, w_hbm, x_hbm, g_hbm, top_hbm, gain_ref, sign_ref, h_ref, inv_hbm, slope_hbm,
    fb_in, go_in, gl_in, gp_in, ga_in,
    next_hbm, fb_out, go_out, gl_out, gp_out, ga_out,
    w_ref, g_ref, x_ref, fb_ref, inv_ref, slope_ref, dn_ref, v_ref, go_ref, next_ref, gp_ref, ga_ref,
    w_sems, sems,
):
    shards = w_hbm.shape[0]
    rows = w_ref.shape[0] // shards
    width = x_ref.shape[1]

    @pl.when(s_ref[0] == 1)
    def _():
        row = pl.multiple_of(s_ref[2], C)
        fb_row = pl.multiple_of(s_ref[3], C)
        slot_row = pl.multiple_of(s_ref[4], 8)
        here = pl.ds(row, C)

        def w_load(i):
            return pltpu.make_async_copy(
                w_hbm.at[i ^ 1, pl.ds(0, rows)], w_ref.at[pl.ds(i * rows, rows)], w_sems.at[i]
            )

        g_load = pltpu.make_async_copy(g_hbm, g_ref, sems.at[0])
        top_load = pltpu.make_async_copy(top_hbm.at[here], g_ref, sems.at[0])
        slope_load = pltpu.make_async_copy(slope_hbm.at[here], slope_ref, sems.at[1])
        inv_load = pltpu.make_async_copy(inv_hbm.at[here], inv_ref, sems.at[2])
        x_load = pltpu.make_async_copy(x_hbm.at[here], x_ref, sems.at[3])
        fb_load = pltpu.make_async_copy(fb_out.at[pl.ds(fb_row, C)], fb_ref, sems.at[4])

        @pl.when(s_ref[1] == 1)
        def _():
            top_load.start()

        @pl.when(s_ref[1] == 0)
        def _():
            g_load.start()

        for i in range(shards):
            w_load(i).start()
        slope_load.start()
        inv_load.start()
        x_load.start()
        fb_load.start()
        g_load.wait()
        grad_act = None
        for i in range(shards):
            cols = slice(i * rows, (i + 1) * rows)
            w_load(i).wait()
            part = dot(g_ref[:, cols], w_ref[cols, :])
            grad_act = part if grad_act is None else grad_act + part
        slope_load.wait()
        inv_load.wait()
        grad_pre = (grad_act * slope_ref[...]).astype(jnp.bfloat16)
        gp_ref[...] = grad_pre
        gp_save = pltpu.make_async_copy(gp_ref, gp_out.at[here], sems.at[5])
        gl_save = pltpu.make_async_copy(g_ref, gl_out.at[here], sems.at[6])
        gp_save.start()
        gl_save.start()
        inv = inv_ref[:, 0:1]
        x_load.wait()
        total = None
        step = 1024
        for i in range(width // step):
            cols = slice(i * step, (i + 1) * step)
            grad_hidden = lax.dot_general(
                grad_pre, w_ref[cols, :], (((1,), (1,)), ((), ())), preferred_element_type=jnp.float32
            )
            normed = x_ref[:, cols].astype(jnp.float32) * inv
            term = grad_hidden * normed
            ga_ref[:, cols] = jnp.sum(term.reshape(C // 8, 8, step), axis=0)
            dn_ref[:, cols] = grad_hidden * gain_ref[:, cols]
            part = jnp.sum(term * gain_ref[:, cols], axis=1, keepdims=True)
            total = part if total is None else total + part
        ga_save = pltpu.make_async_copy(ga_ref, ga_out.at[pl.ds(slot_row, 8)], sems.at[7])
        ga_save.start()
        back = inv * inv * (total / width)
        fb_load.wait()
        per = 8
        matrix = h_ref[...]
        for group in range(width // HB // per):
            for k in range(per):
                b = group * per + k
                cols = slice(b * HB, (b + 1) * HB)
                grad_out = (
                    g_ref[:, cols].astype(jnp.float32)
                    + inv * dn_ref[:, cols]
                    - back * x_ref[:, cols].astype(jnp.float32)
                )
                go_ref[:, cols] = grad_out.astype(jnp.bfloat16)
                value = grad_out + fb_ref[:, cols]
                fb_ref[:, cols] = value
                v_ref[b * C : (b + 1) * C, :] = (value * sign_ref[:, cols]).astype(jnp.bfloat16)
        go_save = pltpu.make_async_copy(go_ref, go_out.at[here], sems.at[8])
        go_save.start()

        @pl.when(s_ref[5] == 1)
        def _():
            for group in range(width // HB // per):
                rotated = dot(v_ref[group * per * C : (group + 1) * per * C, :], matrix)
                scale = jnp.mean(jnp.abs(rotated), axis=1, keepdims=True) + eps_scale
                scale = scale.astype(jnp.bfloat16).astype(jnp.float32)
                levels = jnp.clip(rotated * (1.0 / scale), -1.0, 1.0).astype(jnp.bfloat16)
                decoded = dot(levels, matrix) * scale
                for k in range(per):
                    b = group * per + k
                    cols = slice(b * HB, (b + 1) * HB)
                    back_b = decoded[k * C : (k + 1) * C, :] * sign_ref[:, cols]
                    next_ref[:, cols] = back_b.astype(jnp.bfloat16)
                    fb_ref[:, cols] = fb_ref[:, cols] - back_b
            fb_save = pltpu.make_async_copy(fb_ref, fb_out.at[pl.ds(fb_row, C)], sems.at[9])
            next_save = pltpu.make_async_copy(next_ref, next_hbm, sems.at[10])
            next_save.start()
            fb_save.start()
            next_save.wait()
            fb_save.wait()

        gp_save.wait()
        gl_save.wait()
        ga_save.wait()
        go_save.wait()


def stage(scalars, weight, inputs, grad_in, top, gain, sign, matrix, inv, slope, state):
    width = inputs.shape[1]
    adapter = weight.shape[2]
    f32, bf16 = jnp.float32, jnp.bfloat16
    out = pl.pallas_call(
        stage_kernel,
        in_specs=[SM, ANY, ANY, ANY, ANY, VM, VM, VM, ANY, ANY] + [ANY] * 5,
        out_specs=[ANY] * 6,
        out_shape=[jax.ShapeDtypeStruct((C, width), bf16)]
        + [jax.ShapeDtypeStruct(part.shape, part.dtype) for part in state],
        input_output_aliases={10 + i: 1 + i for i in range(5)},
        scratch_shapes=[
            pltpu.VMEM((width, adapter), bf16),
            pltpu.VMEM((C, width), bf16),
            pltpu.VMEM((C, width), bf16),
            pltpu.VMEM((C, width), f32),
            pltpu.VMEM((C, 128), f32),
            pltpu.VMEM((C, adapter), f32),
            pltpu.VMEM((C, width), f32),
            pltpu.VMEM((C * width // HB, HB), bf16),
            pltpu.VMEM((C, width), bf16),
            pltpu.VMEM((C, width), bf16),
            pltpu.VMEM((C, adapter), bf16),
            pltpu.VMEM((8, width), f32),
            pltpu.SemaphoreType.DMA((weight.shape[0],)),
            pltpu.SemaphoreType.DMA((11,)),
        ],
        compiler_params=pltpu.CompilerParams(vmem_limit_bytes=32 * 1024 * 1024),
        cost_estimate=pl.CostEstimate(
            flops=6 * C * width * adapter, bytes_accessed=16 * 1024 * 1024, transcendentals=0
        ),
        name="stage_part",
    )(scalars, weight, inputs, grad_in, top, gain, sign, matrix, inv, slope, *state)
    return out[0], tuple(out[1:])


def weight_kernel(x_ref, gl_ref, inv_ref, gain_ref, gp_ref, act_ref, out_ref):
    normed = x_ref[...].astype(jnp.float32) * inv_ref[:, 0:1]
    hidden = (normed * gain_ref[...]).astype(jnp.bfloat16)
    dims = (((0,), (0,)), ((), ()))
    total = lax.dot_general(hidden, gp_ref[...], dims, preferred_element_type=jnp.float32)
    total += lax.dot_general(gl_ref[...], act_ref[...], dims, preferred_element_type=jnp.float32)
    out_ref[...] = total.astype(out_ref.dtype)


def weight_partial(inputs, grad_low, inv, gain, grad_pre, act):
    tokens, width = inputs.shape
    adapter = act.shape[1]
    block = 512
    return pl.pallas_call(
        weight_kernel,
        grid=(width // block,),
        in_specs=[
            pl.BlockSpec((tokens, block), lambda i: (0, i)),
            pl.BlockSpec((tokens, block), lambda i: (0, i)),
            pl.BlockSpec((tokens, 128), lambda i: (0, 0)),
            pl.BlockSpec((1, block), lambda i: (0, i)),
            pl.BlockSpec((tokens, adapter), lambda i: (0, 0)),
            pl.BlockSpec((tokens, adapter), lambda i: (0, 0)),
        ],
        out_specs=pl.BlockSpec((block, adapter), lambda i: (i ^ 1, 0)),
        out_shape=jax.ShapeDtypeStruct((width, adapter), jnp.bfloat16),
        compiler_params=pltpu.CompilerParams(vmem_limit_bytes=32 * 1024 * 1024),
        name="weight_part",
    )(inputs, grad_low, inv, gain, grad_pre, act)


def per_device(
    section_inputs, top_grads, weights, norm_gains, feedback, rotation_bits, batch_order
):
    f32, bf16 = jnp.float32, jnp.bfloat16
    micros, tokens, width = section_inputs.shape[1:]
    adapter = weights.shape[2]
    core = lax.axis_index("core")
    section = 2 * lax.axis_index("y") + 1 - core
    level = 7 - section
    swap, hop = swap_pairs(), hop_pairs()

    gain_row = norm_gains[0]
    gain_hi = gain_row.astype(bf16)
    gain_mid = (gain_row - gain_hi.astype(f32)).astype(bf16)
    gain_lo = (gain_row - gain_hi.astype(f32) - gain_mid.astype(f32)).astype(bf16)
    shard = jnp.concatenate(
        [
            weights[0],
            jnp.stack([gain_hi, gain_mid, gain_lo]),
            jnp.zeros((PAD - 3, adapter), bf16),
        ],
        axis=0,
    )
    shard = permuted(shard, swap)
    weight = lax.all_gather(shard, GROUP, axis=0)
    parts = weight[:, adapter : adapter + 3, :].astype(f32)
    gain = parts[:, 0] + parts[:, 1] + parts[:, 2]
    gain = gain.reshape(-1, 2, adapter)[:, ::-1].reshape(1, width)

    inputs = permuted(section_inputs[0].reshape(micros * tokens, width), swap)
    top = permuted(top_grads.reshape(micros * tokens, width), top_pairs())
    carried = permuted(feedback[0].astype(bf16), swap).astype(f32)
    sign = (1 - 2 * lax.dynamic_index_in_dim(rotation_bits, section, 0)).astype(f32)
    matrix = hadamard(HB)

    act, slope, inv = forward(weight, inputs, gain)

    chunks = micros * tokens // C
    per_micro = tokens // C
    state = (
        carried,
        jnp.zeros((micros * tokens, width), bf16),
        jnp.zeros((micros * tokens, width), bf16),
        jnp.zeros((micros * tokens, adapter), bf16),
        jnp.zeros((chunks * 8, width), f32),
    )
    streams = 2
    arrived = [jnp.zeros((C, width), bf16) for _ in range(streams)]
    rounds = chunks // streams
    for tick in range(rounds + 7):
        for stream in range(streams):
            turn = tick - level
            live = jnp.logical_and(turn >= 0, turn < rounds)
            chunk = jnp.clip(turn, 0, rounds - 1) * streams + stream
            micro = lax.dynamic_index_in_dim(batch_order, chunk // per_micro, 0, keepdims=False)
            offset = (chunk % per_micro) * C
            scalars = jnp.stack(
                [
                    live.astype(jnp.int32),
                    (level == 0).astype(jnp.int32),
                    micro * tokens + offset,
                    offset,
                    chunk * 8,
                    (section > 0).astype(jnp.int32),
                    jnp.int32(0),
                    jnp.int32(0),
                ]
            )
            sent, state = stage(
                scalars, weight, inputs, arrived[stream], top, gain, sign, matrix, inv, slope, state
            )
            if tick < rounds + 6:
                arrived[stream] = permuted(sent, hop)
    carried, grads, grad_low, grad_pre, gain_terms = state
    partial = weight_partial(inputs, grad_low, inv, gain, grad_pre, act)
    weight_share = lax.psum_scatter(partial, GROUP, scatter_dimension=0, tiled=True)
    gain_sum = jnp.sum(gain_terms, axis=0)
    gain_all = lax.all_gather(gain_sum, GROUP, axis=0)
    place = lax.axis_index(GROUP) ^ 1
    gain_share = lax.dynamic_slice_in_dim(jnp.sum(gain_all, axis=0), place * adapter, adapter, 0)

    grads = permuted(grads, swap).astype(f32).reshape(micros, tokens, width)
    carried = permuted(carried.astype(bf16), swap).astype(f32)
    weight_share = permuted(weight_share, swap).astype(f32)
    gain_share = permuted(gain_share, swap)
    return (grads[None], weight_share[None], gain_share[None], carried[None])


def solution(mesh):
    fine = Mesh(mesh.devices.reshape(SIZES), AXES)
    return jax.shard_map(
        per_device,
        mesh=fine,
        in_specs=(
            P(SECTION, None, FSDP, None),
            P(None, FSDP, None),
            P(SECTION, FSDP, None),
            P(SECTION, FSDP),
            P(SECTION, FSDP, None),
            P(),
            P(),
        ),
        out_specs=(
            P(SECTION, None, FSDP, None),
            P(SECTION, FSDP, None),
            P(SECTION, FSDP),
            P(SECTION, FSDP, None),
        ),
        check_vma=False,
    )
```

```python
import functools
import itertools

import jax
import jax.numpy as jnp
from jax import lax
from jax.experimental import pallas as pl
from jax.experimental.pallas import tpu as pltpu
from jax.sharding import Mesh
from jax.sharding import PartitionSpec as P

HB = 256
C = 32
STREAMS = 2
UNROLL = 16
GROUP_UNROLL = 4
eps_norm = 1e-05
eps_scale = 1e-06

AXES = ("y", "zl", "x", "zh", "core")
SIZES = (4, 2, 4, 2, 2)
SECTION = ("y", "zl")
FSDP = ("x", "zh", "core")
GROUP = ("x", "zh", "zl")
PAD = 16


def linear(y, zl, x, zh, core):
    return (((y * 2 + zl) * 4 + x) * 2 + zh) * 2 + core


def all_coords():
    return itertools.product(*(range(size) for size in SIZES))


def hop_pairs():
    pairs = []
    for y, zl, x, zh, core in all_coords():
        if core == 0:
            pairs.append((linear(y, zl, x, zh, 0), linear(y, zl, x, zh, 1)))
        elif y > 0:
            pairs.append((linear(y, zl, x, zh, 1), linear(y - 1, zl, x, zh, 0)))
    return pairs


def swap_pairs():
    return [
        (linear(y, zl, x, zh, core), linear(y, 1 - zl, x, zh, 1 - core))
        for y, zl, x, zh, core in all_coords()
        if zl == core
    ]


def top_pairs():
    pairs = []
    for y, zl, x, zh, core in all_coords():
        if y == 3 and zl == 0 and core == 1:
            pairs.append((linear(y, zl, x, zh, 1), linear(y, zl, x, zh, 0)))
        elif y == 3 and zl == 1 and core == 0:
            pairs.append((linear(y, zl, x, zh, 0), linear(y, zl, x, zh, 0)))
    return pairs


def permuted(value, pairs):
    return lax.ppermute(value, AXES, pairs)


def hadamard(order_size):
    position = jnp.arange(order_size, dtype=jnp.int32)
    shared_bits = jnp.bitwise_and(position[:, None], position[None, :])
    parity = jnp.zeros((order_size, order_size), jnp.int32)
    for bit_place in range(order_size.bit_length() - 1):
        parity = parity + jnp.bitwise_and(jnp.right_shift(shared_bits, bit_place), 1)
    return ((1 - 2 * (parity % 2)).astype(jnp.float32) / 16.0).astype(jnp.bfloat16)


def dot(left, right):
    return jnp.dot(left, right, preferred_element_type=jnp.float32)


ANY = pl.BlockSpec(memory_space=pl.ANY)
VM = pl.BlockSpec(memory_space=pltpu.VMEM)
SM = pl.BlockSpec(memory_space=pltpu.SMEM)
HB_SPEC = pl.BlockSpec(memory_space=pltpu.HBM)


def prepare_kernel(
    piece, w_ref, x_own, x_got, fb_own, fb_got, gain_ref,
    x_in, act_in, slope_in, inv_in, fb_in,
    x_ref, act_ref, slope_ref, inv_ref, fb_ref,
    wide_ref, low_ref, sems,
):
    shards = w_ref.shape[0]
    rows = w_ref.shape[2]
    width = x_ref.shape[1]
    span = x_own.shape[0]
    here = pl.ds(piece * span, span)
    keep = lax.axis_index("zl") != lax.axis_index("core")
    with_feedback = (piece + 1) * span <= fb_ref.shape[0]

    def copies(kept):
        x_load = pltpu.make_async_copy(x_own if kept else x_got, x_ref.at[here], sems.at[0])
        if not with_feedback:
            return [x_load]
        source, target = (fb_own, fb_ref.at[here]) if kept else (fb_got, low_ref)
        return [x_load, pltpu.make_async_copy(source, target, sems.at[1])]

    for kept in (True, False):

        @pl.when(keep == kept)
        def _(kept=kept):
            for copy in copies(kept):
                copy.start()
            for copy in copies(kept):
                copy.wait()
            if with_feedback and not kept:
                fb_ref[here, :] = low_ref[...].astype(jnp.float32)

    total = jnp.zeros((span, 128), jnp.float32)
    for i in range(shards):
        part = x_ref[here, i * rows : (i + 1) * rows].astype(jnp.float32)
        part = part * part
        for k in range(rows // 128):
            total = total + part[:, k * 128 : (k + 1) * 128]
    inv = lax.rsqrt(jnp.sum(total, axis=1, keepdims=True) / width + eps_norm)
    inv_ref[here, :] = jnp.broadcast_to(inv, (span, 128))
    pre = jnp.zeros((span, w_ref.shape[2]), jnp.float32)
    for i in range(shards):
        cols = slice(i * rows, (i + 1) * rows)
        hidden = (x_ref[here, cols].astype(jnp.float32) * inv * gain_ref[:, cols]).astype(jnp.bfloat16)
        pre = pre + dot(hidden, w_ref[i ^ 1, 0:rows, :])
    sigma = 1.0 / (1.0 + jnp.exp(-pre))
    act_ref[here, :] = (pre * sigma).astype(jnp.bfloat16)
    slope_ref[here, :] = sigma * (1.0 + pre * (1.0 - sigma))


def prepare(piece, weight, x_own, x_got, fb_own, fb_got, gain, state):
    span, width = x_own.shape
    out = pl.pallas_call(
        functools.partial(prepare_kernel, piece),
        in_specs=[VM] + [HB_SPEC] * 4 + [VM] + [VM] * 5,
        out_specs=[VM] * 5,
        out_shape=[pltpu.VMEM(part.shape, part.dtype) for part in state],
        input_output_aliases={6 + i: i for i in range(5)},
        scratch_shapes=[
            pltpu.VMEM((8, 128), jnp.float32),
            pltpu.VMEM((span, width), jnp.bfloat16),
            pltpu.SemaphoreType.DMA((2,)),
        ],
        compiler_params=pltpu.CompilerParams(vmem_limit_bytes=12 * 1024 * 1024),
        cost_estimate=pl.CostEstimate(
            flops=2 * span * width * 512, bytes_accessed=10 * 1024 * 1024, transcendentals=0
        ),
        name="prepare_part",
    )(
        in_vmem(weight), *[in_hbm(part) for part in (x_own, x_got, fb_own, fb_got)], in_vmem(gain),
        *[in_vmem(part) for part in state],
    )
    return tuple(out)


def transpose_kernel(w_ref, out_ref):
    out_ref[...] = w_ref[0, 0 : out_ref.shape[1], :].T


def transposed(weight):
    shards, _, adapter = weight.shape
    return pl.pallas_call(
        transpose_kernel,
        grid=(shards,),
        in_specs=[pl.BlockSpec((1, weight.shape[1], adapter), lambda i: (i ^ 1, 0, 0))],
        out_specs=pl.BlockSpec((adapter, adapter), lambda i: (0, i)),
        out_shape=jax.ShapeDtypeStruct((adapter, shards * adapter), weight.dtype),
        compiler_params=pltpu.CompilerParams(vmem_limit_bytes=16 * 1024 * 1024),
        name="transpose_part",
    )(weight)


def stage_kernel(
    tick, stream, rounds, top_hbm, w_ref, wt_ref, gain_ref, sign_ref, h_ref,
    g_in, x_in, slope_in, inv_in, fb_in, gp_in, gl_in, ga_in, go_in,
    g_ref, x_ref, slope_ref, inv_ref, fb_ref, gp_ref, gl_ref, ga_ref, go_hbm,
    dn_ref, v_ref, go_ref, sem, go_sem,
):
    shards = w_ref.shape[0]
    rows = w_ref.shape[2]
    width = x_ref.shape[1]
    section = 2 * lax.axis_index("y") + 1 - lax.axis_index("core")
    turn = tick - 7 + section

    @pl.when(jnp.logical_and(turn >= 0, turn < rounds))
    def _():
        chunk = turn * STREAMS + stream
        here = pl.ds(pl.multiple_of(chunk * C, C), C)
        there = pl.ds(pl.multiple_of(lax.rem(chunk, fb_ref.shape[0] // C) * C, C), C)
        slot = pl.ds(pl.multiple_of(chunk * 8, 8), 8)

        @pl.when(section == 7)
        def _():
            top_load = pltpu.make_async_copy(top_hbm.at[here], g_ref, sem)
            top_load.start()
            top_load.wait()

        def low(i, grad_act):
            cols = pl.ds(pl.multiple_of(i * rows, rows), rows)
            low_g = g_ref[:, cols]
            gl_ref[here, cols] = low_g
            return grad_act + dot(low_g, w_ref[i ^ 1, 0:rows, :])

        grad_act = lax.fori_loop(
            0, shards, low, jnp.zeros((C, w_ref.shape[2]), jnp.float32), unroll=UNROLL
        )
        grad_pre = (grad_act * slope_ref[here, :]).astype(jnp.bfloat16)
        gp_ref[here, :] = grad_pre
        inv = inv_ref[here, 0:1]

        def high(i, total):
            cols = pl.ds(pl.multiple_of(i * rows, rows), rows)
            grad_hidden = dot(grad_pre, wt_ref[:, cols])
            term = grad_hidden * (x_ref[here, cols].astype(jnp.float32) * inv)
            ga_ref[slot, cols] = jnp.sum(term.reshape(C // 8, 8, rows), axis=0)
            gain = gain_ref[:, cols]
            dn_ref[:, cols] = grad_hidden * gain
            weighted = term * gain
            for k in range(rows // 128):
                total = total + weighted[:, k * 128 : (k + 1) * 128]
            return total

        total = lax.fori_loop(0, shards, high, jnp.zeros((C, 128), jnp.float32), unroll=UNROLL)
        back = inv * inv * (jnp.sum(total, axis=1, keepdims=True) / width)
        per = 8
        groups = width // HB // per
        matrix = h_ref[...]

        def columns(group, k):
            return pl.ds(pl.multiple_of(group * (per * HB) + k * HB, HB), HB)

        def value_of(group, k):
            cols = columns(group, k)
            grad_out = (
                g_ref[:, cols].astype(jnp.float32)
                + inv * dn_ref[:, cols]
                - back * x_ref[here, cols].astype(jnp.float32)
            )
            go_ref[:, cols] = grad_out.astype(jnp.bfloat16)
            return grad_out

        @pl.when(section == 0)
        def _():
            def plain(group, carry):
                for k in range(per):
                    value_of(group, k)
                return carry

            lax.fori_loop(0, groups, plain, 0)
            pltpu.make_async_copy(go_ref, go_hbm.at[here], go_sem).start()

        @pl.when(section > 0)
        def _():
            def coded(group, carry):
                for k in range(per):
                    cols = columns(group, k)
                    value = value_of(group, k) + fb_ref[there, cols]
                    fb_ref[there, cols] = value
                    v_ref[group, k * C : (k + 1) * C, :] = (value * sign_ref[:, cols]).astype(
                        jnp.bfloat16
                    )
                span = pl.ds(pl.multiple_of(group * (per * HB), HB), per * HB)
                pltpu.make_async_copy(
                    go_ref.at[:, span], go_hbm.at[here, span], go_sem
                ).start()
                rotated = dot(v_ref[group], matrix)
                scale = jnp.mean(jnp.abs(rotated), axis=1, keepdims=True) + eps_scale
                scale = scale.astype(jnp.bfloat16).astype(jnp.float32)
                levels = jnp.clip(rotated * (1.0 / scale), -1.0, 1.0).astype(jnp.bfloat16)
                decoded = dot(levels, matrix) * scale
                for k in range(per):
                    cols = columns(group, k)
                    back_b = decoded[k * C : (k + 1) * C, :] * sign_ref[:, cols]
                    g_ref[:, cols] = back_b.astype(jnp.bfloat16)
                    fb_ref[there, cols] = fb_ref[there, cols] - back_b
                return carry

            lax.fori_loop(0, groups, coded, 0, unroll=GROUP_UNROLL)

        pltpu.make_async_copy(go_ref, go_hbm.at[here], go_sem).wait()


def in_vmem(value):
    return pltpu.with_memory_space_constraint(value, pltpu.VMEM)


def in_hbm(value):
    return pltpu.with_memory_space_constraint(value, pltpu.HBM)


def stage(tick, stream, rounds, top, fixed, grad_in, state):
    width = top.shape[1]
    near = [grad_in, *state[:-1]]
    count = len(near) + 1
    out = pl.pallas_call(
        functools.partial(stage_kernel, tick, stream, rounds),
        in_specs=[HB_SPEC] + [VM] * len(fixed) + [VM] * len(near) + [HB_SPEC],
        out_specs=[VM] * len(near) + [HB_SPEC],
        out_shape=[pltpu.VMEM(part.shape, part.dtype) for part in near]
        + [pltpu.HBM(state[-1].shape, state[-1].dtype)],
        input_output_aliases={1 + len(fixed) + i: i for i in range(count)},
        scratch_shapes=[
            pltpu.VMEM((C, width), jnp.float32),
            pltpu.VMEM((4, C * 8, HB), jnp.bfloat16),
            pltpu.VMEM((C, width), jnp.bfloat16),
            pltpu.SemaphoreType.DMA,
            pltpu.SemaphoreType.DMA,
        ],
        compiler_params=pltpu.CompilerParams(vmem_limit_bytes=12 * 1024 * 1024),
        cost_estimate=pl.CostEstimate(
            flops=6 * C * width * 512, bytes_accessed=16 * 1024 * 1024, transcendentals=0
        ),
        name="stage_part",
    )(
        in_hbm(top), *[in_vmem(part) for part in fixed],
        *[in_vmem(part) for part in near], in_hbm(state[-1]),
    )
    return out[0], tuple(out[1:])


def weight_kernel(x_ref, gl_ref, inv_ref, gain_ref, gp_ref, act_ref, ga_ref, out_hbm, part_ref, sems):
    shards = out_hbm.shape[0]
    rows = act_ref.shape[1]
    inv = inv_ref[:, 0:1]
    dims = (((0,), (0,)), ((), ()))

    def save(i, slot):
        return pltpu.make_async_copy(part_ref.at[slot], out_hbm.at[i ^ 1], sems.at[slot])

    def step(pair, carry):
        for slot in range(2):
            i = pair * 2 + slot

            @pl.when(pair > 0)
            def _():
                save(i - 2, slot).wait()

            cols = pl.ds(pl.multiple_of(i * rows, rows), rows)
            normed = x_ref[:, cols].astype(jnp.float32) * inv
            hidden = (normed * gain_ref[:, cols]).astype(jnp.bfloat16)
            total = lax.dot_general(hidden, gp_ref[...], dims, preferred_element_type=jnp.float32)
            total += lax.dot_general(
                gl_ref[:, cols], act_ref[...], dims, preferred_element_type=jnp.float32
            )
            part_ref[slot, 0:rows, :] = total.astype(jnp.bfloat16)
            gain_sum = jnp.sum(ga_ref[:, cols], axis=0, keepdims=True)
            part_ref[slot, rows : rows + PAD, :] = jnp.broadcast_to(gain_sum, (PAD, rows)).astype(
                jnp.bfloat16
            )
            save(i, slot).start()
        return carry

    lax.fori_loop(0, shards // 2, step, 0)
    for slot in range(2):
        save(shards - 2 + slot, slot).wait()


def weight_partial(inputs, grad_low, inv, gain, grad_pre, act, gain_terms):
    adapter = act.shape[1]
    shards = inputs.shape[1] // adapter
    return pl.pallas_call(
        weight_kernel,
        in_specs=[VM] * 7,
        out_specs=HB_SPEC,
        out_shape=pltpu.HBM((shards, adapter + PAD, adapter), jnp.bfloat16),
        scratch_shapes=[
            pltpu.VMEM((2, adapter + PAD, adapter), jnp.bfloat16),
            pltpu.SemaphoreType.DMA((2,)),
        ],
        compiler_params=pltpu.CompilerParams(vmem_limit_bytes=12 * 1024 * 1024),
        name="weight_part",
    )(*[in_vmem(part) for part in (inputs, grad_low, inv, gain, grad_pre, act, gain_terms)])


def per_device(
    section_inputs, top_grads, weights, norm_gains, feedback, rotation_bits, batch_order
):
    f32, bf16 = jnp.float32, jnp.bfloat16
    micros, tokens, width = section_inputs.shape[1:]
    adapter = weights.shape[2]
    core = lax.axis_index("core")
    keep = lax.axis_index("zl") != core
    section = 2 * lax.axis_index("y") + 1 - core
    swap, hop = swap_pairs(), hop_pairs()

    def swapped(value):
        return permuted(value, swap)

    gain_row = norm_gains[0]
    gain_hi = gain_row.astype(bf16)
    gain_mid = (gain_row - gain_hi.astype(f32)).astype(bf16)
    gain_lo = (gain_row - gain_hi.astype(f32) - gain_mid.astype(f32)).astype(bf16)
    shard = jnp.concatenate(
        [
            weights[0],
            jnp.stack([gain_hi, gain_mid, gain_lo]),
            jnp.zeros((PAD - 3, adapter), bf16),
        ],
        axis=0,
    )
    shard = jnp.where(keep, shard, swapped(shard))
    weight = lax.all_gather(shard, GROUP, axis=0)
    parts = weight[:, adapter : adapter + 3, :].astype(f32)
    gain = parts[:, 0] + parts[:, 1] + parts[:, 2]
    gain = gain.reshape(-1, 2, adapter)[:, ::-1].reshape(1, width)

    span = C * STREAMS
    rounds = micros * tokens // span
    per_micro = tokens // span
    own, got, fb_own, fb_got = [], [], [], []
    for piece in range(rounds):
        micro = batch_order[piece // per_micro]
        start = (piece % per_micro) * span
        part = lax.dynamic_slice(section_inputs[0], (micro, start, 0), (1, span, width))[0]
        own.append(part)
        if piece < per_micro:
            fb_own.append(feedback[0, start : start + span])
        if piece >= 2:
            part, _ = lax.optimization_barrier((part, weight[0, 0, 0]))
        got.append(swapped(part))
        if piece < per_micro:
            fb_got.append(swapped(fb_own[piece].astype(bf16)))
    top = jnp.where(batch_order[0] == 0, top_grads, top_grads[::-1])
    top = permuted(top.reshape(micros * tokens, width), top_pairs())
    sign = (1 - 2 * lax.dynamic_index_in_dim(rotation_bits, section, 0)).astype(f32)
    matrix = hadamard(HB)
    chunks = rounds * STREAMS

    inputs = jnp.full((micros * tokens, width), 1.0, bf16)
    act = jnp.zeros((micros * tokens, adapter), bf16)
    slope = jnp.zeros((micros * tokens, adapter), f32)
    inv = jnp.zeros((micros * tokens, 128), f32)
    carried = jnp.zeros((tokens, width), f32)
    grad_pre = jnp.full((micros * tokens, adapter), 1.0, bf16)
    grad_low = jnp.full((micros * tokens, width), 2.0, bf16)
    gain_terms = jnp.zeros((chunks * 8, width), f32)
    grads = jnp.full((micros * tokens, width), 3.0, bf16)
    fixed = (weight, transposed(weight), gain, sign, matrix)
    arrived = [jnp.full((C, width), 4.0 + stream, bf16) for stream in range(STREAMS)]
    ticks = rounds + 7
    for tick in range(ticks):
        if tick < rounds:
            last = min(tick, per_micro - 1)
            inputs, act, slope, inv, carried = prepare(
                tick, weight, own[tick], got[tick], fb_own[last], fb_got[last], gain,
                (inputs, act, slope, inv, carried),
            )
        for stream in range(STREAMS):
            state = (inputs, slope, inv, carried, grad_pre, grad_low, gain_terms, grads)
            sent, state = stage(tick, stream, rounds, top, fixed, arrived[stream], state)
            inputs, slope, inv, carried, grad_pre, grad_low, gain_terms, grads = state
            if tick < ticks - 1:
                arrived[stream] = permuted(sent, hop)
    partial = weight_partial(inputs, grad_low, inv, gain, grad_pre, act, gain_terms)
    share = lax.psum_scatter(
        partial.reshape(-1, adapter), GROUP, scatter_dimension=0, tiled=True
    )
    grads = jnp.where(keep, grads, swapped(grads)).reshape(micros, tokens, width)
    grads = jnp.where(batch_order[0] == 0, grads, grads[::-1]).astype(f32)
    carried = jnp.where(keep, carried, swapped(carried.astype(bf16)).astype(f32))
    share = jnp.where(keep, share, swapped(share)).astype(f32)
    return (grads[None], share[None, :adapter], share[None, adapter], carried[None])


def solution(mesh):
    fine = Mesh(mesh.devices.reshape(SIZES), AXES)
    return jax.shard_map(
        per_device,
        mesh=fine,
        in_specs=(
            P(SECTION, None, FSDP, None),
            P(None, FSDP, None),
            P(SECTION, FSDP, None),
            P(SECTION, FSDP),
            P(SECTION, FSDP, None),
            P(),
            P(),
        ),
        out_specs=(
            P(SECTION, None, FSDP, None),
            P(SECTION, FSDP, None),
            P(SECTION, FSDP),
            P(SECTION, FSDP, None),
        ),
        check_vma=False,
    )
```

```python
import functools
import itertools

import jax
import jax.numpy as jnp
from jax import lax
from jax.experimental import pallas as pl
from jax.experimental.pallas import tpu as pltpu
from jax.sharding import Mesh
from jax.sharding import PartitionSpec as P

HB = 256
C = 32
STREAMS = 2
UNROLL = 16
GROUP_UNROLL = 4
eps_norm = 1e-05
eps_scale = 1e-06

AXES = ("y", "zl", "x", "zh", "core")
SIZES = (4, 2, 4, 2, 2)
SECTION = ("y", "zl")
FSDP = ("x", "zh", "core")
GROUP = ("x", "zh", "zl")
PAD = 16


def linear(y, zl, x, zh, core):
    return (((y * 2 + zl) * 4 + x) * 2 + zh) * 2 + core


def all_coords():
    return itertools.product(*(range(size) for size in SIZES))


def hop_pairs():
    pairs = []
    for y, zl, x, zh, core in all_coords():
        if core == 0:
            pairs.append((linear(y, zl, x, zh, 0), linear(y, zl, x, zh, 1)))
        elif y > 0:
            pairs.append((linear(y, zl, x, zh, 1), linear(y - 1, zl, x, zh, 0)))
    return pairs


def swap_pairs():
    return [
        (linear(y, zl, x, zh, core), linear(y, 1 - zl, x, zh, 1 - core))
        for y, zl, x, zh, core in all_coords()
        if zl == core
    ]


def top_pairs():
    pairs = []
    for y, zl, x, zh, core in all_coords():
        if y == 3 and zl == 0 and core == 1:
            pairs.append((linear(y, zl, x, zh, 1), linear(y, zl, x, zh, 0)))
        elif y == 3 and zl == 1 and core == 0:
            pairs.append((linear(y, zl, x, zh, 0), linear(y, zl, x, zh, 0)))
    return pairs


def permuted(value, pairs):
    return lax.ppermute(value, AXES, pairs)


def hadamard(order_size):
    position = jnp.arange(order_size, dtype=jnp.int32)
    shared_bits = jnp.bitwise_and(position[:, None], position[None, :])
    parity = jnp.zeros((order_size, order_size), jnp.int32)
    for bit_place in range(order_size.bit_length() - 1):
        parity = parity + jnp.bitwise_and(jnp.right_shift(shared_bits, bit_place), 1)
    return ((1 - 2 * (parity % 2)).astype(jnp.float32) / 16.0).astype(jnp.bfloat16)


def dot(left, right):
    return jnp.dot(left, right, preferred_element_type=jnp.float32)


ANY = pl.BlockSpec(memory_space=pl.ANY)
VM = pl.BlockSpec(memory_space=pltpu.VMEM)
SM = pl.BlockSpec(memory_space=pltpu.SMEM)
HB_SPEC = pl.BlockSpec(memory_space=pltpu.HBM)


def prepare_kernel(piece, w_ref, x_own, x_got, fb_own, fb_got, gain_ref, *rest):
    low_ref, sems = rest[-2:]
    x_ref, act_ref, slope_ref, inv_ref, fb_ref = rest[0 if piece == 0 else 5 :][:5]
    shards = w_ref.shape[0]
    rows = w_ref.shape[2]
    width = x_ref.shape[1]
    span = x_own.shape[0]
    here = pl.ds(piece * span, span)
    keep = lax.axis_index("zl") != lax.axis_index("core")
    with_feedback = (piece + 1) * span <= fb_ref.shape[0]

    def copies(kept):
        x_load = pltpu.make_async_copy(x_own if kept else x_got, x_ref.at[here], sems.at[0])
        if not with_feedback:
            return [x_load]
        source, target = (fb_own, fb_ref.at[here]) if kept else (fb_got, low_ref)
        return [x_load, pltpu.make_async_copy(source, target, sems.at[1])]

    for kept in (True, False):

        @pl.when(keep == kept)
        def _(kept=kept):
            for copy in copies(kept):
                copy.start()
            for copy in copies(kept):
                copy.wait()
            if with_feedback and not kept:
                fb_ref[here, :] = low_ref[...].astype(jnp.float32)

    total = jnp.zeros((span, 128), jnp.float32)
    for i in range(shards):
        part = x_ref[here, i * rows : (i + 1) * rows].astype(jnp.float32)
        part = part * part
        for k in range(rows // 128):
            total = total + part[:, k * 128 : (k + 1) * 128]
    inv = lax.rsqrt(jnp.sum(total, axis=1, keepdims=True) / width + eps_norm)
    inv_ref[here, :] = jnp.broadcast_to(inv, (span, 128))
    pre = jnp.zeros((span, w_ref.shape[2]), jnp.float32)
    for i in range(shards):
        cols = slice(i * rows, (i + 1) * rows)
        hidden = (x_ref[here, cols].astype(jnp.float32) * inv * gain_ref[:, cols]).astype(jnp.bfloat16)
        pre = pre + dot(hidden, w_ref[i])
    sigma = 1.0 / (1.0 + jnp.exp(-pre))
    act_ref[here, :] = (pre * sigma).astype(jnp.bfloat16)
    slope_ref[here, :] = sigma * (1.0 + pre * (1.0 - sigma))


def prepare(piece, weight, x_own, x_got, fb_own, fb_got, gain, state, fresh=()):
    span, width = x_own.shape
    count = len(state)
    out = pl.pallas_call(
        functools.partial(prepare_kernel, piece),
        in_specs=[VM] + [HB_SPEC] * 4 + [VM] + [VM] * count,
        out_specs=[VM] * (count + len(fresh)),
        out_shape=[pltpu.VMEM(part.shape, part.dtype) for part in (*state, *fresh)],
        input_output_aliases={6 + i: i for i in range(count)},
        scratch_shapes=[
            pltpu.VMEM((span, width), jnp.bfloat16),
            pltpu.SemaphoreType.DMA((2,)),
        ],
        compiler_params=pltpu.CompilerParams(vmem_limit_bytes=12 * 1024 * 1024),
        cost_estimate=pl.CostEstimate(
            flops=2 * span * width * 512, bytes_accessed=10 * 1024 * 1024, transcendentals=0
        ),
        name="prepare_part",
    )(
        in_vmem(weight), *[in_hbm(part) for part in (x_own, x_got, fb_own, fb_got)], in_vmem(gain),
        *[in_vmem(part) for part in state],
    )
    return tuple(out)


def load_kernel(gathered, w_ref, wt_ref, gain_ref, extra_ref, sems):
    shards, rows, _ = w_ref.shape

    def copies(i):
        return [
            pltpu.make_async_copy(gathered.at[i ^ 1, pl.ds(0, rows)], w_ref.at[i], sems.at[0, i]),
            pltpu.make_async_copy(gathered.at[i ^ 1, pl.ds(rows, PAD)], extra_ref.at[i], sems.at[1, i]),
        ]

    for i in range(shards):
        for copy in copies(i):
            copy.start()
    for i in range(shards):
        for copy in copies(i):
            copy.wait()
        cols = slice(i * rows, (i + 1) * rows)
        wt_ref[:, cols] = w_ref[i].T
        extra = extra_ref[i].astype(jnp.float32)
        gain_ref[:, cols] = extra[0:1] + extra[1:2] + extra[2:3]


def load(gathered):
    shards, rows, adapter = gathered.shape
    rows -= PAD
    bf16 = jnp.bfloat16
    return pl.pallas_call(
        load_kernel,
        in_specs=[HB_SPEC],
        out_specs=[VM] * 3,
        out_shape=[
            pltpu.VMEM((shards, rows, adapter), bf16),
            pltpu.VMEM((adapter, shards * rows), bf16),
            pltpu.VMEM((1, shards * rows), jnp.float32),
        ],
        scratch_shapes=[
            pltpu.VMEM((shards, PAD, adapter), bf16),
            pltpu.SemaphoreType.DMA((2, shards)),
        ],
        compiler_params=pltpu.CompilerParams(vmem_limit_bytes=12 * 1024 * 1024),
        name="load_part",
    )(in_hbm(gathered))


def in_vmem(value):
    return pltpu.with_memory_space_constraint(value, pltpu.VMEM)


def in_hbm(value):
    return pltpu.with_memory_space_constraint(value, pltpu.HBM)


def stage_kernel(
    tick, stream, rounds, top_hbm, w_ref, wt_ref, gain_ref, sign_ref, h_ref,
    *rest,
):
    dn_ref, v_ref, go_ref, sem, go_sem = rest[-5:]
    g_ref, x_ref, slope_ref, inv_ref, fb_ref, gp_ref, gl_ref, ga_ref, go_hbm = rest[-14:-5]
    shards = w_ref.shape[0]
    rows = w_ref.shape[2]
    width = x_ref.shape[1]
    section = 2 * lax.axis_index("y") + 1 - lax.axis_index("core")
    turn = tick - 7 + section

    @pl.when(jnp.logical_and(turn >= 0, turn < rounds))
    def _():
        chunk = turn * STREAMS + stream
        here = pl.ds(pl.multiple_of(chunk * C, C), C)
        there = pl.ds(pl.multiple_of(lax.rem(chunk, fb_ref.shape[0] // C) * C, C), C)
        slot = pl.ds(pl.multiple_of(chunk * 8, 8), 8)
        share = pl.ds(stream * C, C)

        @pl.when(section == 7)
        def _():
            top_load = pltpu.make_async_copy(top_hbm.at[here], g_ref, sem)
            top_load.start()
            top_load.wait()

        def low(i, grad_act):
            cols = pl.ds(pl.multiple_of(i * rows, rows), rows)
            low_g = g_ref[:, cols]
            gl_ref[here, cols] = low_g
            return grad_act + dot(low_g, w_ref[i])

        grad_act = lax.fori_loop(
            0, shards, low, jnp.zeros((C, w_ref.shape[2]), jnp.float32), unroll=UNROLL
        )
        grad_pre = (grad_act * slope_ref[here, :]).astype(jnp.bfloat16)
        gp_ref[here, :] = grad_pre
        inv = inv_ref[here, 0:1]

        def high(i, total):
            cols = pl.ds(pl.multiple_of(i * rows, rows), rows)
            grad_hidden = dot(grad_pre, wt_ref[:, cols])
            term = grad_hidden * (x_ref[here, cols].astype(jnp.float32) * inv)
            ga_ref[slot, cols] = jnp.sum(term.reshape(C // 8, 8, rows), axis=0)
            gain = gain_ref[:, cols]
            dn_ref[:, cols] = grad_hidden * gain
            weighted = term * gain
            for k in range(rows // 128):
                total = total + weighted[:, k * 128 : (k + 1) * 128]
            return total

        total = lax.fori_loop(0, shards, high, jnp.zeros((C, 128), jnp.float32), unroll=UNROLL)
        back = inv * inv * (jnp.sum(total, axis=1, keepdims=True) / width)
        per = 8
        groups = width // HB // per
        matrix = h_ref[...]

        def columns(group, k):
            return pl.ds(pl.multiple_of(group * (per * HB) + k * HB, HB), HB)

        def value_of(group, k):
            cols = columns(group, k)
            grad_out = (
                g_ref[:, cols].astype(jnp.float32)
                + inv * dn_ref[:, cols]
                - back * x_ref[here, cols].astype(jnp.float32)
            )
            go_ref[:, cols] = grad_out.astype(jnp.bfloat16)
            return grad_out

        @pl.when(section == 0)
        def _():
            def plain(group, carry):
                for k in range(per):
                    value_of(group, k)
                return carry

            lax.fori_loop(0, groups, plain, 0)
            pltpu.make_async_copy(go_ref, go_hbm.at[share], go_sem).start()

        @pl.when(section > 0)
        def _():
            def coded(group, carry):
                for k in range(per):
                    cols = columns(group, k)
                    value = value_of(group, k) + fb_ref[there, cols]
                    fb_ref[there, cols] = value
                    v_ref[group, k * C : (k + 1) * C, :] = (value * sign_ref[:, cols]).astype(
                        jnp.bfloat16
                    )
                span = pl.ds(pl.multiple_of(group * (per * HB), HB), per * HB)
                pltpu.make_async_copy(
                    go_ref.at[:, span], go_hbm.at[share, span], go_sem
                ).start()
                rotated = dot(v_ref[group], matrix)
                scale = jnp.mean(jnp.abs(rotated), axis=1, keepdims=True) + eps_scale
                scale = scale.astype(jnp.bfloat16).astype(jnp.float32)
                levels = jnp.clip(rotated * (1.0 / scale), -1.0, 1.0).astype(jnp.bfloat16)
                decoded = dot(levels, matrix) * scale
                for k in range(per):
                    cols = columns(group, k)
                    back_b = decoded[k * C : (k + 1) * C, :] * sign_ref[:, cols]
                    g_ref[:, cols] = back_b.astype(jnp.bfloat16)
                    fb_ref[there, cols] = fb_ref[there, cols] - back_b
                return carry

            lax.fori_loop(0, groups, coded, 0, unroll=GROUP_UNROLL)

        pltpu.make_async_copy(go_ref, go_hbm.at[share], go_sem).wait()


def stage(tick, stream, rounds, top, fixed, grad_in, state, piece):
    width = top.shape[1]
    near = [grad_in, *state]
    count = len(near)
    before = [] if piece is None else [in_hbm(piece)]
    aliases = {1 + len(fixed) + i: i for i in range(count + len(before))}
    out = pl.pallas_call(
        functools.partial(stage_kernel, tick, stream, rounds),
        in_specs=[HB_SPEC] + [VM] * (len(fixed) + count) + [HB_SPEC] * len(before),
        out_specs=[VM] * count + [HB_SPEC],
        out_shape=[pltpu.VMEM(part.shape, part.dtype) for part in near]
        + [pltpu.HBM((STREAMS * C, width), jnp.bfloat16)],
        input_output_aliases=aliases,
        scratch_shapes=[
            pltpu.VMEM((C, width), jnp.float32),
            pltpu.VMEM((4, C * 8, HB), jnp.bfloat16),
            pltpu.VMEM((C, width), jnp.bfloat16),
            pltpu.SemaphoreType.DMA,
            pltpu.SemaphoreType.DMA,
        ],
        compiler_params=pltpu.CompilerParams(vmem_limit_bytes=12 * 1024 * 1024),
        cost_estimate=pl.CostEstimate(
            flops=6 * C * width * 512, bytes_accessed=16 * 1024 * 1024, transcendentals=0
        ),
        name="stage_part",
    )(
        in_hbm(top), *[in_vmem(part) for part in fixed],
        *[in_vmem(part) for part in near], *before,
    )
    return out[0], tuple(out[1:-1]), out[-1]


def collect_kernel(order_ref, *rest):
    low_ref, wide_ref, in_sems, out_sems = rest[-4:]
    out_hbm = rest[-5]
    pieces = rest[:-5]
    ticks = len(pieces) // 2
    micros, tokens, _ = out_hbm.shape
    span = low_ref.shape[1]
    per_micro = tokens // span
    rounds = micros * per_micro
    core = lax.axis_index("core")
    keep = lax.axis_index("zl") != core
    level = 6 - 2 * lax.axis_index("y") + jnp.where(keep, core, 1 - core)

    def fetch(turn):
        for at_level in range(ticks - rounds + 1):
            for kept in (True, False):

                @pl.when(jnp.logical_and(level == at_level, keep == kept))
                def _(at_level=at_level, kept=kept):
                    source = pieces[turn + at_level + (0 if kept else ticks)]
                    pltpu.make_async_copy(source, low_ref.at[turn], in_sems.at[turn]).start()

    def save(turn):
        start = (turn % per_micro) * span
        return pltpu.make_async_copy(
            wide_ref.at[turn % 2],
            out_hbm.at[order_ref[turn // per_micro], pl.ds(start, span)],
            out_sems.at[turn % 2],
        )

    for turn in range(rounds):
        fetch(turn)
    for turn in range(rounds):
        pltpu.make_async_copy(pieces[0], low_ref.at[turn], in_sems.at[turn]).wait()
        if turn >= 2:
            save(turn - 2).wait()
        wide_ref[turn % 2] = low_ref[turn].astype(jnp.float32)
        save(turn).start()
    save(rounds - 2).wait()
    save(rounds - 1).wait()


def collect(order, pieces, micros, tokens):
    span, width = pieces[0].shape
    rounds = micros * tokens // span
    return pl.pallas_call(
        collect_kernel,
        in_specs=[SM] + [HB_SPEC] * len(pieces),
        out_specs=HB_SPEC,
        out_shape=pltpu.HBM((micros, tokens, width), jnp.float32),
        scratch_shapes=[
            pltpu.VMEM((rounds, span, width), jnp.bfloat16),
            pltpu.VMEM((2, span, width), jnp.float32),
            pltpu.SemaphoreType.DMA((rounds,)),
            pltpu.SemaphoreType.DMA((2,)),
        ],
        compiler_params=pltpu.CompilerParams(vmem_limit_bytes=12 * 1024 * 1024),
        name="collect_part",
    )(order, *[in_hbm(part) for part in pieces])


def weight_kernel(x_ref, gl_ref, inv_ref, gain_ref, gp_ref, act_ref, ga_ref, out_hbm, part_ref, sems):
    shards = out_hbm.shape[0]
    rows = act_ref.shape[1]
    inv = inv_ref[:, 0:1]
    dims = (((0,), (0,)), ((), ()))

    def save(i, slot):
        return pltpu.make_async_copy(part_ref.at[slot], out_hbm.at[i ^ 1], sems.at[slot])

    def step(pair, carry):
        for slot in range(2):
            i = pair * 2 + slot

            @pl.when(pair > 0)
            def _():
                save(i - 2, slot).wait()

            cols = pl.ds(pl.multiple_of(i * rows, rows), rows)
            normed = x_ref[:, cols].astype(jnp.float32) * inv
            hidden = (normed * gain_ref[:, cols]).astype(jnp.bfloat16)
            total = lax.dot_general(hidden, gp_ref[...], dims, preferred_element_type=jnp.float32)
            total += lax.dot_general(
                gl_ref[:, cols], act_ref[...], dims, preferred_element_type=jnp.float32
            )
            part_ref[slot, 0:rows, :] = total.astype(jnp.bfloat16)
            gain_sum = jnp.sum(ga_ref[:, cols], axis=0, keepdims=True)
            part_ref[slot, rows : rows + PAD, :] = jnp.broadcast_to(gain_sum, (PAD, rows)).astype(
                jnp.bfloat16
            )
            save(i, slot).start()
        return carry

    lax.fori_loop(0, shards // 2, step, 0)
    for slot in range(2):
        save(shards - 2 + slot, slot).wait()


def weight_partial(inputs, grad_low, inv, gain, grad_pre, act, gain_terms):
    adapter = act.shape[1]
    shards = inputs.shape[1] // adapter
    return pl.pallas_call(
        weight_kernel,
        in_specs=[VM] * 7,
        out_specs=HB_SPEC,
        out_shape=pltpu.HBM((shards, adapter + PAD, adapter), jnp.bfloat16),
        scratch_shapes=[
            pltpu.VMEM((2, adapter + PAD, adapter), jnp.bfloat16),
            pltpu.SemaphoreType.DMA((2,)),
        ],
        compiler_params=pltpu.CompilerParams(vmem_limit_bytes=12 * 1024 * 1024),
        name="weight_part",
    )(*[in_vmem(part) for part in (inputs, grad_low, inv, gain, grad_pre, act, gain_terms)])


def per_device(
    section_inputs, top_grads, weights, norm_gains, feedback, rotation_bits, batch_order
):
    f32, bf16 = jnp.float32, jnp.bfloat16
    micros, tokens, width = section_inputs.shape[1:]
    adapter = weights.shape[2]
    core = lax.axis_index("core")
    keep = lax.axis_index("zl") != core
    section = 2 * lax.axis_index("y") + 1 - core
    swap, hop = swap_pairs(), hop_pairs()

    def swapped(value):
        return permuted(value, swap)

    gain_row = norm_gains[0]
    gain_hi = gain_row.astype(bf16)
    gain_mid = (gain_row - gain_hi.astype(f32)).astype(bf16)
    gain_lo = (gain_row - gain_hi.astype(f32) - gain_mid.astype(f32)).astype(bf16)
    shard = jnp.concatenate(
        [
            weights[0],
            jnp.stack([gain_hi, gain_mid, gain_lo]),
            jnp.zeros((PAD - 3, adapter), bf16),
        ],
        axis=0,
    )
    shard = jnp.where(keep, shard, swapped(shard))
    gathered = lax.all_gather(shard, GROUP, axis=0)
    weight, weight_t, gain = load(gathered)

    span = C * STREAMS
    rounds = micros * tokens // span
    per_micro = tokens // span
    own, got, fb_own, fb_got = [], [], [], []
    for piece in range(rounds):
        micro = batch_order[piece // per_micro]
        start = (piece % per_micro) * span
        part = lax.dynamic_slice(section_inputs[0], (micro, start, 0), (1, span, width))[0]
        own.append(part)
        if piece < per_micro:
            fb_own.append(feedback[0, start : start + span])
        if piece >= 1:
            part, _ = lax.optimization_barrier((part, gathered[0, 0, 0]))
        got.append(swapped(part))
        if piece < per_micro:
            part = fb_own[piece].astype(bf16)
            if piece >= 1:
                part, _ = lax.optimization_barrier((part, gathered[0, 0, 0]))
            fb_got.append(swapped(part))
    top = jnp.where(batch_order[0] == 0, top_grads, top_grads[::-1])
    top = permuted(top.reshape(micros * tokens, width), top_pairs())
    sign = (1 - 2 * lax.dynamic_index_in_dim(rotation_bits, section, 0)).astype(f32)
    matrix = hadamard(HB)
    chunks = rounds * STREAMS

    def blank(rows, cols, dtype):
        return jax.ShapeDtypeStruct((rows, cols), dtype)

    rows = micros * tokens
    fresh = [
        blank(rows, width, bf16),
        blank(rows, adapter, bf16),
        blank(rows, adapter, f32),
        blank(rows, 128, f32),
        blank(tokens, width, f32),
        blank(rows, adapter, bf16),
        blank(rows, width, bf16),
        blank(chunks * 8, width, f32),
    ] + [blank(C, width, bf16)] * STREAMS
    fixed = (weight, weight_t, gain, sign, matrix)
    ticks = rounds + 7
    pieces, pieces_got = [], []
    for tick in range(ticks):
        if tick < rounds:
            last = min(tick, per_micro - 1)
            ready = prepare(
                tick, weight, own[tick], got[tick], fb_own[last], fb_got[last], gain,
                () if tick == 0 else (inputs, act, slope, inv, carried),
                fresh if tick == 0 else (),
            )
            inputs, act, slope, inv, carried = ready[:5]
            if tick == 0:
                grad_pre, grad_low, gain_terms = ready[5:8]
                arrived = list(ready[8:])
        piece = None
        if tick >= 2:
            arrived[0], pieces_got[tick - 2] = lax.optimization_barrier(
                (arrived[0], pieces_got[tick - 2])
            )
        for stream in range(STREAMS):
            state = (inputs, slope, inv, carried, grad_pre, grad_low, gain_terms)
            sent, state, piece = stage(
                tick, stream, rounds, top, fixed, arrived[stream], state, piece
            )
            inputs, slope, inv, carried, grad_pre, grad_low, gain_terms = state
            if tick < ticks - 1:
                arrived[stream] = permuted(sent, hop)
        pieces.append(piece)
        pieces_got.append(swapped(piece))
    partial = weight_partial(inputs, grad_low, inv, gain, grad_pre, act, gain_terms)
    share = lax.psum_scatter(
        partial.reshape(-1, adapter), GROUP, scatter_dimension=0, tiled=True
    )
    grads = collect(batch_order, pieces + pieces_got, micros, tokens)
    carried = jnp.where(keep, carried, swapped(carried.astype(bf16)).astype(f32))
    share = jnp.where(keep, share, swapped(share)).astype(f32)
    return (grads[None], share[None, :adapter], share[None, adapter], carried[None])


def solution(mesh):
    fine = Mesh(mesh.devices.reshape(SIZES), AXES)
    return jax.shard_map(
        per_device,
        mesh=fine,
        in_specs=(
            P(SECTION, None, FSDP, None),
            P(None, FSDP, None),
            P(SECTION, FSDP, None),
            P(SECTION, FSDP),
            P(SECTION, FSDP, None),
            P(),
            P(),
        ),
        out_specs=(
            P(SECTION, None, FSDP, None),
            P(SECTION, FSDP, None),
            P(SECTION, FSDP),
            P(SECTION, FSDP, None),
        ),
        check_vma=False,
    )
```

```python
import functools
import itertools

import jax
import jax.numpy as jnp
from jax import lax
from jax.experimental import pallas as pl
from jax.experimental.pallas import tpu as pltpu
from jax.sharding import Mesh
from jax.sharding import PartitionSpec as P

HB = 256
C = 32
STREAMS = 2
UNROLL = 16
GROUP_UNROLL = 4
eps_norm = 1e-05
eps_scale = 1e-06

AXES = ("y", "zl", "x", "zh", "core")
SIZES = (4, 2, 4, 2, 2)
SECTION = ("y", "zl")
FSDP = ("x", "zh", "core")
GROUP = ("x", "zh", "zl")
PAD = 16


def linear(y, zl, x, zh, core):
    return (((y * 2 + zl) * 4 + x) * 2 + zh) * 2 + core


def all_coords():
    return itertools.product(*(range(size) for size in SIZES))


def hop_pairs():
    pairs = []
    for y, zl, x, zh, core in all_coords():
        if core == 0:
            pairs.append((linear(y, zl, x, zh, 0), linear(y, zl, x, zh, 1)))
        elif y > 0:
            pairs.append((linear(y, zl, x, zh, 1), linear(y - 1, zl, x, zh, 0)))
    return pairs


def swap_pairs():
    return [
        (linear(y, zl, x, zh, core), linear(y, 1 - zl, x, zh, 1 - core))
        for y, zl, x, zh, core in all_coords()
        if zl == core
    ]


def top_pairs():
    pairs = []
    for y, zl, x, zh, core in all_coords():
        if y == 3 and zl == 0 and core == 1:
            pairs.append((linear(y, zl, x, zh, 1), linear(y, zl, x, zh, 0)))
        elif y == 3 and zl == 1 and core == 0:
            pairs.append((linear(y, zl, x, zh, 0), linear(y, zl, x, zh, 0)))
    return pairs


def permuted(value, pairs):
    return lax.ppermute(value, AXES, pairs)


def hadamard(order_size):
    position = jnp.arange(order_size, dtype=jnp.int32)
    shared_bits = jnp.bitwise_and(position[:, None], position[None, :])
    parity = jnp.zeros((order_size, order_size), jnp.int32)
    for bit_place in range(order_size.bit_length() - 1):
        parity = parity + jnp.bitwise_and(jnp.right_shift(shared_bits, bit_place), 1)
    return ((1 - 2 * (parity % 2)).astype(jnp.float32) / 16.0).astype(jnp.bfloat16)


def dot(left, right):
    return jnp.dot(left, right, preferred_element_type=jnp.float32)


ANY = pl.BlockSpec(memory_space=pl.ANY)
VM = pl.BlockSpec(memory_space=pltpu.VMEM)
SM = pl.BlockSpec(memory_space=pltpu.SMEM)
HB_SPEC = pl.BlockSpec(memory_space=pltpu.HBM)


def prepare_kernel(piece, w_ref, x_own, x_got, fb_own, fb_got, gain_ref, *rest):
    low_ref, sems = rest[-2:]
    x_ref, act_ref, slope_ref, inv_ref, fb_ref = rest[0 if piece == 0 else 5 :][:5]
    shards = w_ref.shape[0]
    rows = w_ref.shape[2]
    width = x_ref.shape[1]
    span = x_own.shape[0]
    here = pl.ds(piece * span, span)
    keep = lax.axis_index("zl") != lax.axis_index("core")
    with_feedback = (piece + 1) * span <= fb_ref.shape[0]

    def copies(kept):
        x_load = pltpu.make_async_copy(x_own if kept else x_got, x_ref.at[here], sems.at[0])
        if not with_feedback:
            return [x_load]
        source, target = (fb_own, fb_ref.at[here]) if kept else (fb_got, low_ref)
        return [x_load, pltpu.make_async_copy(source, target, sems.at[1])]

    for kept in (True, False):

        @pl.when(keep == kept)
        def _(kept=kept):
            for copy in copies(kept):
                copy.start()
            for copy in copies(kept):
                copy.wait()
            if with_feedback and not kept:
                fb_ref[here, :] = low_ref[...].astype(jnp.float32)

    total = jnp.zeros((span, 128), jnp.float32)
    for i in range(shards):
        part = x_ref[here, i * rows : (i + 1) * rows].astype(jnp.float32)
        part = part * part
        for k in range(rows // 128):
            total = total + part[:, k * 128 : (k + 1) * 128]
    inv = lax.rsqrt(jnp.sum(total, axis=1, keepdims=True) / width + eps_norm)
    inv_ref[here, :] = jnp.broadcast_to(inv, (span, 128))
    pre = jnp.zeros((span, w_ref.shape[2]), jnp.float32)
    for i in range(shards):
        cols = slice(i * rows, (i + 1) * rows)
        hidden = (x_ref[here, cols].astype(jnp.float32) * inv * gain_ref[:, cols]).astype(jnp.bfloat16)
        pre = pre + dot(hidden, w_ref[i])
    sigma = 1.0 / (1.0 + jnp.exp(-pre))
    act_ref[here, :] = (pre * sigma).astype(jnp.bfloat16)
    slope_ref[here, :] = sigma * (1.0 + pre * (1.0 - sigma))


def prepare(piece, weight, x_own, x_got, fb_own, fb_got, gain, state, fresh=()):
    span, width = x_own.shape
    count = len(state)
    out = pl.pallas_call(
        functools.partial(prepare_kernel, piece),
        in_specs=[VM] + [HB_SPEC] * 4 + [VM] + [VM] * count,
        out_specs=[VM] * (count + len(fresh)),
        out_shape=[pltpu.VMEM(part.shape, part.dtype) for part in (*state, *fresh)],
        input_output_aliases={6 + i: i for i in range(count)},
        scratch_shapes=[
            pltpu.VMEM((span, width), jnp.bfloat16),
            pltpu.SemaphoreType.DMA((2,)),
        ],
        compiler_params=pltpu.CompilerParams(vmem_limit_bytes=12 * 1024 * 1024),
        cost_estimate=pl.CostEstimate(
            flops=2 * span * width * 512, bytes_accessed=10 * 1024 * 1024, transcendentals=0
        ),
        name="prepare_part",
    )(
        in_vmem(weight), *[in_hbm(part) for part in (x_own, x_got, fb_own, fb_got)], in_vmem(gain),
        *[in_vmem(part) for part in state],
    )
    return tuple(out)


def load_kernel(gathered, w_ref, wt_ref, gain_ref, extra_ref, sems):
    shards, rows, _ = w_ref.shape

    def copies(i):
        return [
            pltpu.make_async_copy(gathered.at[i ^ 1, pl.ds(0, rows)], w_ref.at[i], sems.at[0, i]),
            pltpu.make_async_copy(gathered.at[i ^ 1, pl.ds(rows, PAD)], extra_ref.at[i], sems.at[1, i]),
        ]

    for i in range(shards):
        for copy in copies(i):
            copy.start()
    for i in range(shards):
        for copy in copies(i):
            copy.wait()
        cols = slice(i * rows, (i + 1) * rows)
        wt_ref[:, cols] = w_ref[i].T
        extra = extra_ref[i].astype(jnp.float32)
        gain_ref[:, cols] = extra[0:1] + extra[1:2] + extra[2:3]


def load(gathered):
    shards, rows, adapter = gathered.shape
    rows -= PAD
    bf16 = jnp.bfloat16
    return pl.pallas_call(
        load_kernel,
        in_specs=[HB_SPEC],
        out_specs=[VM] * 3,
        out_shape=[
            pltpu.VMEM((shards, rows, adapter), bf16),
            pltpu.VMEM((adapter, shards * rows), bf16),
            pltpu.VMEM((1, shards * rows), jnp.float32),
        ],
        scratch_shapes=[
            pltpu.VMEM((shards, PAD, adapter), bf16),
            pltpu.SemaphoreType.DMA((2, shards)),
        ],
        compiler_params=pltpu.CompilerParams(vmem_limit_bytes=12 * 1024 * 1024),
        name="load_part",
    )(in_hbm(gathered))


def in_vmem(value):
    return pltpu.with_memory_space_constraint(value, pltpu.VMEM)


def in_hbm(value):
    return pltpu.with_memory_space_constraint(value, pltpu.HBM)


def stage_kernel(
    tick, stream, rounds, top_hbm, w_ref, wt_ref, gain_ref, sign_ref, h_ref,
    *rest,
):
    dn_ref, v_ref, go_ref, sem, go_sem = rest[-5:]
    g_ref, x_ref, slope_ref, inv_ref, fb_ref, gp_ref, gl_ref, ga_ref, go_hbm = rest[-14:-5]
    shards = w_ref.shape[0]
    rows = w_ref.shape[2]
    width = x_ref.shape[1]
    section = 2 * lax.axis_index("y") + 1 - lax.axis_index("core")
    turn = tick - 7 + section

    @pl.when(jnp.logical_and(turn >= 0, turn < rounds))
    def _():
        chunk = turn * STREAMS + stream
        here = pl.ds(pl.multiple_of(chunk * C, C), C)
        there = pl.ds(pl.multiple_of(lax.rem(chunk, fb_ref.shape[0] // C) * C, C), C)
        slot = pl.ds(pl.multiple_of(chunk * 8, 8), 8)
        share = pl.ds(stream * C, C)

        @pl.when(section == 7)
        def _():
            top_load = pltpu.make_async_copy(top_hbm.at[here], g_ref, sem)
            top_load.start()
            top_load.wait()

        def low(i, grad_act):
            cols = pl.ds(pl.multiple_of(i * rows, rows), rows)
            low_g = g_ref[:, cols]
            gl_ref[here, cols] = low_g
            return grad_act + dot(low_g, w_ref[i])

        grad_act = lax.fori_loop(
            0, shards, low, jnp.zeros((C, w_ref.shape[2]), jnp.float32), unroll=UNROLL
        )
        grad_pre = (grad_act * slope_ref[here, :]).astype(jnp.bfloat16)
        gp_ref[here, :] = grad_pre
        inv = inv_ref[here, 0:1]

        def high(i, total):
            cols = pl.ds(pl.multiple_of(i * rows, rows), rows)
            grad_hidden = dot(grad_pre, wt_ref[:, cols])
            term = grad_hidden * (x_ref[here, cols].astype(jnp.float32) * inv)
            ga_ref[slot, cols] = jnp.sum(term.reshape(C // 8, 8, rows), axis=0)
            gain = gain_ref[:, cols]
            dn_ref[:, cols] = grad_hidden * gain
            weighted = term * gain
            for k in range(rows // 128):
                total = total + weighted[:, k * 128 : (k + 1) * 128]
            return total

        total = lax.fori_loop(0, shards, high, jnp.zeros((C, 128), jnp.float32), unroll=UNROLL)
        back = inv * inv * (jnp.sum(total, axis=1, keepdims=True) / width)
        per = 8
        groups = width // HB // per
        matrix = h_ref[...]

        def columns(group, k):
            return pl.ds(pl.multiple_of(group * (per * HB) + k * HB, HB), HB)

        def value_of(group, k):
            cols = columns(group, k)
            grad_out = (
                g_ref[:, cols].astype(jnp.float32)
                + inv * dn_ref[:, cols]
                - back * x_ref[here, cols].astype(jnp.float32)
            )
            go_ref[:, cols] = grad_out.astype(jnp.bfloat16)
            return grad_out

        @pl.when(section == 0)
        def _():
            def plain(group, carry):
                for k in range(per):
                    value_of(group, k)
                return carry

            lax.fori_loop(0, groups, plain, 0)
            pltpu.make_async_copy(go_ref, go_hbm.at[share], go_sem).start()

        @pl.when(section > 0)
        def _():
            def coded(group, carry):
                for k in range(per):
                    cols = columns(group, k)
                    value = value_of(group, k) + fb_ref[there, cols]
                    fb_ref[there, cols] = value
                    v_ref[group, k * C : (k + 1) * C, :] = (value * sign_ref[:, cols]).astype(
                        jnp.bfloat16
                    )
                span = pl.ds(pl.multiple_of(group * (per * HB), HB), per * HB)
                pltpu.make_async_copy(
                    go_ref.at[:, span], go_hbm.at[share, span], go_sem
                ).start()
                rotated = dot(v_ref[group], matrix)
                scale = jnp.mean(jnp.abs(rotated), axis=1, keepdims=True) + eps_scale
                scale = scale.astype(jnp.bfloat16).astype(jnp.float32)
                levels = jnp.clip(rotated * (1.0 / scale), -1.0, 1.0).astype(jnp.bfloat16)
                decoded = dot(levels, matrix) * scale
                for k in range(per):
                    cols = columns(group, k)
                    back_b = decoded[k * C : (k + 1) * C, :] * sign_ref[:, cols]
                    g_ref[:, cols] = back_b.astype(jnp.bfloat16)
                    fb_ref[there, cols] = fb_ref[there, cols] - back_b
                return carry

            lax.fori_loop(0, groups, coded, 0, unroll=GROUP_UNROLL)

        pltpu.make_async_copy(go_ref, go_hbm.at[share], go_sem).wait()


def stage(tick, stream, rounds, top, fixed, grad_in, state, piece):
    width = top.shape[1]
    near = [grad_in, *state]
    count = len(near)
    before = [] if piece is None else [in_hbm(piece)]
    aliases = {1 + len(fixed) + i: i for i in range(count + len(before))}
    out = pl.pallas_call(
        functools.partial(stage_kernel, tick, stream, rounds),
        in_specs=[HB_SPEC] + [VM] * (len(fixed) + count) + [HB_SPEC] * len(before),
        out_specs=[VM] * count + [HB_SPEC],
        out_shape=[pltpu.VMEM(part.shape, part.dtype) for part in near]
        + [pltpu.HBM((STREAMS * C, width), jnp.bfloat16)],
        input_output_aliases=aliases,
        scratch_shapes=[
            pltpu.VMEM((C, width), jnp.float32),
            pltpu.VMEM((4, C * 8, HB), jnp.bfloat16),
            pltpu.VMEM((C, width), jnp.bfloat16),
            pltpu.SemaphoreType.DMA,
            pltpu.SemaphoreType.DMA,
        ],
        compiler_params=pltpu.CompilerParams(vmem_limit_bytes=12 * 1024 * 1024),
        cost_estimate=pl.CostEstimate(
            flops=6 * C * width * 512, bytes_accessed=16 * 1024 * 1024, transcendentals=0
        ),
        name="stage_part",
    )(
        in_hbm(top), *[in_vmem(part) for part in fixed],
        *[in_vmem(part) for part in near], *before,
    )
    return out[0], tuple(out[1:-1]), out[-1]


def collect_kernel(order_ref, *rest):
    low_ref, wide_ref, in_sems, out_sems = rest[-4:]
    out_hbm = rest[-5]
    pieces = rest[:-5]
    ticks = len(pieces) // 2
    micros, tokens, _ = out_hbm.shape
    span = low_ref.shape[1]
    per_micro = tokens // span
    rounds = micros * per_micro
    core = lax.axis_index("core")
    keep = lax.axis_index("zl") != core
    level = 6 - 2 * lax.axis_index("y") + jnp.where(keep, core, 1 - core)

    def fetch(turn):
        for at_level in range(ticks - rounds + 1):
            for kept in (True, False):

                @pl.when(jnp.logical_and(level == at_level, keep == kept))
                def _(at_level=at_level, kept=kept):
                    source = pieces[turn + at_level + (0 if kept else ticks)]
                    pltpu.make_async_copy(source, low_ref.at[turn], in_sems.at[turn]).start()

    def save(turn):
        start = (turn % per_micro) * span
        return pltpu.make_async_copy(
            wide_ref.at[turn % 2],
            out_hbm.at[order_ref[turn // per_micro], pl.ds(start, span)],
            out_sems.at[turn % 2],
        )

    for turn in range(rounds):
        fetch(turn)
    for turn in range(rounds):
        pltpu.make_async_copy(pieces[0], low_ref.at[turn], in_sems.at[turn]).wait()
        if turn >= 2:
            save(turn - 2).wait()
        wide_ref[turn % 2] = low_ref[turn].astype(jnp.float32)
        save(turn).start()
    save(rounds - 2).wait()
    save(rounds - 1).wait()


def collect(order, pieces, micros, tokens):
    span, width = pieces[0].shape
    rounds = micros * tokens // span
    return pl.pallas_call(
        collect_kernel,
        in_specs=[SM] + [HB_SPEC] * len(pieces),
        out_specs=HB_SPEC,
        out_shape=pltpu.HBM((micros, tokens, width), jnp.float32),
        scratch_shapes=[
            pltpu.VMEM((rounds, span, width), jnp.bfloat16),
            pltpu.VMEM((2, span, width), jnp.float32),
            pltpu.SemaphoreType.DMA((rounds,)),
            pltpu.SemaphoreType.DMA((2,)),
        ],
        compiler_params=pltpu.CompilerParams(vmem_limit_bytes=12 * 1024 * 1024),
        name="collect_part",
    )(order, *[in_hbm(part) for part in pieces])


def weight_kernel(
    x_ref, gl_ref, inv_ref, gain_ref, gp_ref, act_ref, ga_ref, out_hbm, left_ref, right_ref, part_ref, sems
):
    shards = out_hbm.shape[0]
    rows = act_ref.shape[1]
    inv = inv_ref[:, 0:1]
    dims = (((0,), (0,)), ((), ()))
    tokens = x_ref.shape[0]
    slots = part_ref.shape[0]
    right_ref[0:tokens, :] = gp_ref[...]
    right_ref[tokens:, :] = act_ref[...]

    def save(i, slot):
        return pltpu.make_async_copy(part_ref.at[slot], out_hbm.at[i ^ 1], sems.at[slot])

    def step(turn, carry):
        for slot in range(slots):
            i = turn * slots + slot

            @pl.when(turn > 0)
            def _():
                save(i - slots, slot).wait()

            cols = pl.ds(pl.multiple_of(i * rows, rows), rows)
            normed = x_ref[:, cols].astype(jnp.float32) * inv
            hidden = (normed * gain_ref[:, cols]).astype(jnp.bfloat16)
            left_ref[slot, 0:tokens, :] = hidden
            left_ref[slot, tokens:, :] = gl_ref[:, cols]
            total = lax.dot_general(
                left_ref[slot], right_ref[...], dims, preferred_element_type=jnp.float32
            )
            part_ref[slot, 0:rows, :] = total.astype(jnp.bfloat16)
            gain_sum = jnp.sum(ga_ref[:, cols], axis=0, keepdims=True)
            part_ref[slot, rows : rows + PAD, :] = jnp.broadcast_to(gain_sum, (PAD, rows)).astype(
                jnp.bfloat16
            )
            save(i, slot).start()
        return carry

    lax.fori_loop(0, shards // slots, step, 0)
    for slot in range(slots):
        save(shards - slots + slot, slot).wait()


def weight_partial(inputs, grad_low, inv, gain, grad_pre, act, gain_terms):
    adapter = act.shape[1]
    shards = inputs.shape[1] // adapter
    return pl.pallas_call(
        weight_kernel,
        in_specs=[VM] * 7,
        out_specs=HB_SPEC,
        out_shape=pltpu.HBM((shards, adapter + PAD, adapter), jnp.bfloat16),
        scratch_shapes=[
            pltpu.VMEM((4, 2 * inputs.shape[0], adapter), jnp.bfloat16),
            pltpu.VMEM((2 * inputs.shape[0], adapter), jnp.bfloat16),
            pltpu.VMEM((4, adapter + PAD, adapter), jnp.bfloat16),
            pltpu.SemaphoreType.DMA((4,)),
        ],
        compiler_params=pltpu.CompilerParams(vmem_limit_bytes=12 * 1024 * 1024),
        name="weight_part",
    )(*[in_vmem(part) for part in (inputs, grad_low, inv, gain, grad_pre, act, gain_terms)])


def per_device(
    section_inputs, top_grads, weights, norm_gains, feedback, rotation_bits, batch_order
):
    f32, bf16 = jnp.float32, jnp.bfloat16
    micros, tokens, width = section_inputs.shape[1:]
    adapter = weights.shape[2]
    core = lax.axis_index("core")
    keep = lax.axis_index("zl") != core
    section = 2 * lax.axis_index("y") + 1 - core
    swap, hop = swap_pairs(), hop_pairs()

    def swapped(value):
        return permuted(value, swap)

    gain_row = norm_gains[0]
    gain_hi = gain_row.astype(bf16)
    gain_mid = (gain_row - gain_hi.astype(f32)).astype(bf16)
    gain_lo = (gain_row - gain_hi.astype(f32) - gain_mid.astype(f32)).astype(bf16)
    shard = jnp.concatenate(
        [
            weights[0],
            jnp.stack([gain_hi, gain_mid, gain_lo]),
            jnp.zeros((PAD - 3, adapter), bf16),
        ],
        axis=0,
    )
    shard = jnp.where(keep, shard, swapped(shard))
    gathered = lax.all_gather(shard, GROUP, axis=0)
    weight, weight_t, gain = load(gathered)

    span = C * STREAMS
    rounds = micros * tokens // span
    per_micro = tokens // span
    own, got, fb_own, fb_got = [], [], [], []
    for piece in range(rounds):
        micro = batch_order[piece // per_micro]
        start = (piece % per_micro) * span
        part = lax.dynamic_slice(section_inputs[0], (micro, start, 0), (1, span, width))[0]
        own.append(part)
        if piece < per_micro:
            fb_own.append(feedback[0, start : start + span])
        if piece >= 1:
            part, _ = lax.optimization_barrier((part, gathered[0, 0, 0]))
        got.append(swapped(part))
        if piece < per_micro:
            part = fb_own[piece].astype(bf16)
            if piece >= 1:
                part, _ = lax.optimization_barrier((part, gathered[0, 0, 0]))
            fb_got.append(swapped(part))
    top = jnp.where(batch_order[0] == 0, top_grads, top_grads[::-1])
    top = permuted(top.reshape(micros * tokens, width), top_pairs())
    sign = (1 - 2 * lax.dynamic_index_in_dim(rotation_bits, section, 0)).astype(f32)
    matrix = hadamard(HB)
    chunks = rounds * STREAMS

    def blank(rows, cols, dtype):
        return jax.ShapeDtypeStruct((rows, cols), dtype)

    rows = micros * tokens
    fresh = [
        blank(rows, width, bf16),
        blank(rows, adapter, bf16),
        blank(rows, adapter, f32),
        blank(rows, 128, f32),
        blank(tokens, width, f32),
        blank(rows, adapter, bf16),
        blank(rows, width, bf16),
        blank(chunks * 8, width, f32),
    ] + [blank(C, width, bf16)] * STREAMS
    fixed = (weight, weight_t, gain, sign, matrix)
    ticks = rounds + 7
    pieces, pieces_got = [], []
    for tick in range(ticks):
        if tick < rounds:
            last = min(tick, per_micro - 1)
            ready = prepare(
                tick, weight, own[tick], got[tick], fb_own[last], fb_got[last], gain,
                () if tick == 0 else (inputs, act, slope, inv, carried),
                fresh if tick == 0 else (),
            )
            inputs, act, slope, inv, carried = ready[:5]
            if tick == 0:
                grad_pre, grad_low, gain_terms = ready[5:8]
                arrived = list(ready[8:])
        piece = None
        if tick >= 2:
            arrived[0], pieces_got[tick - 2] = lax.optimization_barrier(
                (arrived[0], pieces_got[tick - 2])
            )
        for stream in range(STREAMS):
            state = (inputs, slope, inv, carried, grad_pre, grad_low, gain_terms)
            sent, state, piece = stage(
                tick, stream, rounds, top, fixed, arrived[stream], state, piece
            )
            inputs, slope, inv, carried, grad_pre, grad_low, gain_terms = state
            if tick < ticks - 1:
                arrived[stream] = permuted(sent, hop)
        pieces.append(piece)
        pieces_got.append(swapped(piece))
    pieces_got[-2], gain_terms = lax.optimization_barrier((pieces_got[-2], gain_terms))
    partial = weight_partial(inputs, grad_low, inv, gain, grad_pre, act, gain_terms)
    share = lax.psum_scatter(
        partial.reshape(-1, adapter), GROUP, scatter_dimension=0, tiled=True
    )
    grads = collect(batch_order, pieces + pieces_got, micros, tokens)
    carried = jnp.where(keep, carried, swapped(carried.astype(bf16)).astype(f32))
    share = jnp.where(keep, share, swapped(share)).astype(f32)
    return (grads[None], share[None, :adapter], share[None, adapter], carried[None])


def solution(mesh):
    fine = Mesh(mesh.devices.reshape(SIZES), AXES)
    return jax.shard_map(
        per_device,
        mesh=fine,
        in_specs=(
            P(SECTION, None, FSDP, None),
            P(None, FSDP, None),
            P(SECTION, FSDP, None),
            P(SECTION, FSDP),
            P(SECTION, FSDP, None),
            P(),
            P(),
        ),
        out_specs=(
            P(SECTION, None, FSDP, None),
            P(SECTION, FSDP, None),
            P(SECTION, FSDP),
            P(SECTION, FSDP, None),
        ),
        check_vma=False,
    )
```

```python
import functools
import itertools

import jax
import jax.numpy as jnp
from jax import lax
from jax.experimental import pallas as pl
from jax.experimental.pallas import tpu as pltpu
from jax.sharding import Mesh
from jax.sharding import PartitionSpec as P

HB = 256
C = 32
STREAMS = 2
UNROLL = 16
GROUP_UNROLL = 4
eps_norm = 1e-05
eps_scale = 1e-06

AXES = ("y", "zl", "x", "zh", "core")
SIZES = (4, 2, 4, 2, 2)
SECTION = ("y", "zl")
FSDP = ("x", "zh", "core")
GROUP = ("x", "zh", "zl")
PAD = 16


def linear(y, zl, x, zh, core):
    return (((y * 2 + zl) * 4 + x) * 2 + zh) * 2 + core


def all_coords():
    return itertools.product(*(range(size) for size in SIZES))


def hop_pairs():
    pairs = []
    for y, zl, x, zh, core in all_coords():
        if core == 0:
            pairs.append((linear(y, zl, x, zh, 0), linear(y, zl, x, zh, 1)))
        elif y > 0:
            pairs.append((linear(y, zl, x, zh, 1), linear(y - 1, zl, x, zh, 0)))
    return pairs


def swap_pairs():
    return [
        (linear(y, zl, x, zh, core), linear(y, 1 - zl, x, zh, 1 - core))
        for y, zl, x, zh, core in all_coords()
        if zl == core
    ]


def top_pairs():
    pairs = []
    for y, zl, x, zh, core in all_coords():
        if y == 3 and zl == 0 and core == 1:
            pairs.append((linear(y, zl, x, zh, 1), linear(y, zl, x, zh, 0)))
        elif y == 3 and zl == 1 and core == 0:
            pairs.append((linear(y, zl, x, zh, 0), linear(y, zl, x, zh, 0)))
    return pairs


def permuted(value, pairs):
    return lax.ppermute(value, AXES, pairs)


def hadamard(order_size):
    position = jnp.arange(order_size, dtype=jnp.int32)
    shared_bits = jnp.bitwise_and(position[:, None], position[None, :])
    parity = jnp.zeros((order_size, order_size), jnp.int32)
    for bit_place in range(order_size.bit_length() - 1):
        parity = parity + jnp.bitwise_and(jnp.right_shift(shared_bits, bit_place), 1)
    return ((1 - 2 * (parity % 2)).astype(jnp.float32) / 16.0).astype(jnp.bfloat16)


def dot(left, right):
    return jnp.dot(left, right, preferred_element_type=jnp.float32)


ANY = pl.BlockSpec(memory_space=pl.ANY)
VM = pl.BlockSpec(memory_space=pltpu.VMEM)
SM = pl.BlockSpec(memory_space=pltpu.SMEM)
HB_SPEC = pl.BlockSpec(memory_space=pltpu.HBM)


def prepare_kernel(piece, w_ref, x_own, x_got, fb_own, fb_got, gain_ref, *rest):
    low_ref, sems = rest[-2:]
    x_ref, act_ref, slope_ref, inv_ref, fb_ref = rest[0 if piece == 0 else 5 :][:5]
    shards = w_ref.shape[0]
    rows = w_ref.shape[2]
    width = x_ref.shape[1]
    span = x_own.shape[0]
    here = pl.ds(piece * span, span)
    keep = lax.axis_index("zl") != lax.axis_index("core")
    with_feedback = (piece + 1) * span <= fb_ref.shape[0]

    def copies(kept):
        x_load = pltpu.make_async_copy(x_own if kept else x_got, x_ref.at[here], sems.at[0])
        if not with_feedback:
            return [x_load]
        source, target = (fb_own, fb_ref.at[here]) if kept else (fb_got, low_ref)
        return [x_load, pltpu.make_async_copy(source, target, sems.at[1])]

    for kept in (True, False):

        @pl.when(keep == kept)
        def _(kept=kept):
            for copy in copies(kept):
                copy.start()
            for copy in copies(kept):
                copy.wait()
            if with_feedback and not kept:
                fb_ref[here, :] = low_ref[...].astype(jnp.float32)

    total = jnp.zeros((span, 128), jnp.float32)
    for i in range(shards):
        part = x_ref[here, i * rows : (i + 1) * rows].astype(jnp.float32)
        part = part * part
        for k in range(rows // 128):
            total = total + part[:, k * 128 : (k + 1) * 128]
    inv = lax.rsqrt(jnp.sum(total, axis=1, keepdims=True) / width + eps_norm)
    inv_ref[here, :] = jnp.broadcast_to(inv, (span, 128))
    pre = jnp.zeros((span, w_ref.shape[2]), jnp.float32)
    for i in range(shards):
        cols = slice(i * rows, (i + 1) * rows)
        hidden = (x_ref[here, cols].astype(jnp.float32) * inv * gain_ref[:, cols]).astype(jnp.bfloat16)
        pre = pre + dot(hidden, w_ref[i])
    sigma = 1.0 / (1.0 + jnp.exp(-pre))
    act_ref[here, :] = (pre * sigma).astype(jnp.bfloat16)
    slope_ref[here, :] = sigma * (1.0 + pre * (1.0 - sigma))


def prepare(piece, weight, x_own, x_got, fb_own, fb_got, gain, state, fresh=()):
    span, width = x_own.shape
    count = len(state)
    out = pl.pallas_call(
        functools.partial(prepare_kernel, piece),
        in_specs=[VM] + [HB_SPEC] * 4 + [VM] + [VM] * count,
        out_specs=[VM] * (count + len(fresh)),
        out_shape=[pltpu.VMEM(part.shape, part.dtype) for part in (*state, *fresh)],
        input_output_aliases={6 + i: i for i in range(count)},
        scratch_shapes=[
            pltpu.VMEM((span, width), jnp.bfloat16),
            pltpu.SemaphoreType.DMA((2,)),
        ],
        compiler_params=pltpu.CompilerParams(vmem_limit_bytes=12 * 1024 * 1024),
        cost_estimate=pl.CostEstimate(
            flops=2 * span * width * 512, bytes_accessed=10 * 1024 * 1024, transcendentals=0
        ),
        name="prepare_part",
    )(
        in_vmem(weight), *[in_hbm(part) for part in (x_own, x_got, fb_own, fb_got)], in_vmem(gain),
        *[in_vmem(part) for part in state],
    )
    return tuple(out)


def load_kernel(gathered, w_ref, wt_ref, gain_ref, extra_ref, sems):
    shards, rows, _ = w_ref.shape

    def copies(i):
        return [
            pltpu.make_async_copy(gathered.at[i ^ 1, pl.ds(0, rows)], w_ref.at[i], sems.at[0, i]),
            pltpu.make_async_copy(gathered.at[i ^ 1, pl.ds(rows, PAD)], extra_ref.at[i], sems.at[1, i]),
        ]

    for i in range(shards):
        for copy in copies(i):
            copy.start()
    for i in range(shards):
        for copy in copies(i):
            copy.wait()
        cols = slice(i * rows, (i + 1) * rows)
        wt_ref[:, cols] = w_ref[i].T
        extra = extra_ref[i].astype(jnp.float32)
        gain_ref[:, cols] = extra[0:1] + extra[1:2] + extra[2:3]


def load(gathered):
    shards, rows, adapter = gathered.shape
    rows -= PAD
    bf16 = jnp.bfloat16
    return pl.pallas_call(
        load_kernel,
        in_specs=[HB_SPEC],
        out_specs=[VM] * 3,
        out_shape=[
            pltpu.VMEM((shards, rows, adapter), bf16),
            pltpu.VMEM((adapter, shards * rows), bf16),
            pltpu.VMEM((1, shards * rows), jnp.float32),
        ],
        scratch_shapes=[
            pltpu.VMEM((shards, PAD, adapter), bf16),
            pltpu.SemaphoreType.DMA((2, shards)),
        ],
        compiler_params=pltpu.CompilerParams(vmem_limit_bytes=12 * 1024 * 1024),
        name="load_part",
    )(in_hbm(gathered))


def in_vmem(value):
    return pltpu.with_memory_space_constraint(value, pltpu.VMEM)


def in_hbm(value):
    return pltpu.with_memory_space_constraint(value, pltpu.HBM)


def stage_kernel(
    tick, stream, rounds, top_hbm, w_ref, wt_ref, gain_ref, sign_ref, h_ref,
    *rest,
):
    dn_ref, v_ref, go_ref, sem, go_sem = rest[-5:]
    g_ref, x_ref, slope_ref, inv_ref, fb_ref, gp_ref, gl_ref, ga_ref, go_hbm = rest[-14:-5]
    shards = w_ref.shape[0]
    rows = w_ref.shape[2]
    width = x_ref.shape[1]
    section = 2 * lax.axis_index("y") + 1 - lax.axis_index("core")
    turn = tick - 7 + section

    @pl.when(jnp.logical_and(turn >= 0, turn < rounds))
    def _():
        chunk = turn * STREAMS + stream
        here = pl.ds(pl.multiple_of(chunk * C, C), C)
        there = pl.ds(pl.multiple_of(lax.rem(chunk, fb_ref.shape[0] // C) * C, C), C)
        slot = pl.ds(pl.multiple_of(chunk * 8, 8), 8)
        share = pl.ds(stream * C, C)

        @pl.when(section == 7)
        def _():
            top_load = pltpu.make_async_copy(top_hbm.at[here], g_ref, sem)
            top_load.start()
            top_load.wait()

        def low(i, grad_act):
            cols = pl.ds(pl.multiple_of(i * rows, rows), rows)
            low_g = g_ref[:, cols]
            gl_ref[here, cols] = low_g
            return grad_act + dot(low_g, w_ref[i])

        grad_act = lax.fori_loop(
            0, shards, low, jnp.zeros((C, w_ref.shape[2]), jnp.float32), unroll=UNROLL
        )
        grad_pre = (grad_act * slope_ref[here, :]).astype(jnp.bfloat16)
        gp_ref[here, :] = grad_pre
        inv = inv_ref[here, 0:1]

        def high(i, total):
            cols = pl.ds(pl.multiple_of(i * rows, rows), rows)
            grad_hidden = dot(grad_pre, wt_ref[:, cols])
            term = grad_hidden * (x_ref[here, cols].astype(jnp.float32) * inv)
            ga_ref[slot, cols] = jnp.sum(term.reshape(C // 8, 8, rows), axis=0)
            gain = gain_ref[:, cols]
            dn_ref[:, cols] = grad_hidden * gain
            weighted = term * gain
            for k in range(rows // 128):
                total = total + weighted[:, k * 128 : (k + 1) * 128]
            return total

        total = lax.fori_loop(0, shards, high, jnp.zeros((C, 128), jnp.float32), unroll=UNROLL)
        back = inv * inv * (jnp.sum(total, axis=1, keepdims=True) / width)
        per = 8
        groups = width // HB // per
        matrix = h_ref[...]

        def columns(group, k):
            return pl.ds(pl.multiple_of(group * (per * HB) + k * HB, HB), HB)

        def value_of(group, k):
            cols = columns(group, k)
            grad_out = (
                g_ref[:, cols].astype(jnp.float32)
                + inv * dn_ref[:, cols]
                - back * x_ref[here, cols].astype(jnp.float32)
            )
            go_ref[:, cols] = grad_out.astype(jnp.bfloat16)
            return grad_out

        @pl.when(section == 0)
        def _():
            def plain(group, carry):
                for k in range(per):
                    value_of(group, k)
                return carry

            lax.fori_loop(0, groups, plain, 0)
            pltpu.make_async_copy(go_ref, go_hbm.at[share], go_sem).start()

        @pl.when(section > 0)
        def _():
            def coded(group, carry):
                for k in range(per):
                    cols = columns(group, k)
                    value = value_of(group, k) + fb_ref[there, cols]
                    fb_ref[there, cols] = value
                    v_ref[group, k * C : (k + 1) * C, :] = (value * sign_ref[:, cols]).astype(
                        jnp.bfloat16
                    )
                span = pl.ds(pl.multiple_of(group * (per * HB), HB), per * HB)
                pltpu.make_async_copy(
                    go_ref.at[:, span], go_hbm.at[share, span], go_sem
                ).start()
                rotated = dot(v_ref[group], matrix)
                scale = jnp.mean(jnp.abs(rotated), axis=1, keepdims=True) + eps_scale
                scale = scale.astype(jnp.bfloat16).astype(jnp.float32)
                levels = jnp.clip(rotated * (1.0 / scale), -1.0, 1.0).astype(jnp.bfloat16)
                decoded = dot(levels, matrix) * scale
                for k in range(per):
                    cols = columns(group, k)
                    back_b = decoded[k * C : (k + 1) * C, :] * sign_ref[:, cols]
                    g_ref[:, cols] = back_b.astype(jnp.bfloat16)
                    fb_ref[there, cols] = fb_ref[there, cols] - back_b
                return carry

            lax.fori_loop(0, groups, coded, 0, unroll=GROUP_UNROLL)

        pltpu.make_async_copy(go_ref, go_hbm.at[share], go_sem).wait()


def stage(tick, stream, rounds, top, fixed, grad_in, state, piece):
    width = top.shape[1]
    near = [grad_in, *state]
    count = len(near)
    before = [] if piece is None else [in_hbm(piece)]
    aliases = {1 + len(fixed) + i: i for i in range(count + len(before))}
    out = pl.pallas_call(
        functools.partial(stage_kernel, tick, stream, rounds),
        in_specs=[HB_SPEC] + [VM] * (len(fixed) + count) + [HB_SPEC] * len(before),
        out_specs=[VM] * count + [HB_SPEC],
        out_shape=[pltpu.VMEM(part.shape, part.dtype) for part in near]
        + [pltpu.HBM((STREAMS * C, width), jnp.bfloat16)],
        input_output_aliases=aliases,
        scratch_shapes=[
            pltpu.VMEM((C, width), jnp.float32),
            pltpu.VMEM((4, C * 8, HB), jnp.bfloat16),
            pltpu.VMEM((C, width), jnp.bfloat16),
            pltpu.SemaphoreType.DMA,
            pltpu.SemaphoreType.DMA,
        ],
        compiler_params=pltpu.CompilerParams(vmem_limit_bytes=12 * 1024 * 1024),
        cost_estimate=pl.CostEstimate(
            flops=6 * C * width * 512, bytes_accessed=16 * 1024 * 1024, transcendentals=0
        ),
        name="stage_part",
    )(
        in_hbm(top), *[in_vmem(part) for part in fixed],
        *[in_vmem(part) for part in near], *before,
    )
    return out[0], tuple(out[1:-1]), out[-1]


def collect_kernel(order_ref, *rest):
    low_ref, wide_ref, in_sems, out_sems = rest[-4:]
    out_hbm = rest[-5]
    pieces = rest[:-5]
    ticks = len(pieces) // 2
    micros, tokens, _ = out_hbm.shape
    span = low_ref.shape[1]
    per_micro = tokens // span
    rounds = micros * per_micro
    core = lax.axis_index("core")
    keep = lax.axis_index("zl") != core
    level = 6 - 2 * lax.axis_index("y") + jnp.where(keep, core, 1 - core)

    def fetch(turn):
        for at_level in range(ticks - rounds + 1):
            for kept in (True, False):

                @pl.when(jnp.logical_and(level == at_level, keep == kept))
                def _(at_level=at_level, kept=kept):
                    source = pieces[turn + at_level + (0 if kept else ticks)]
                    pltpu.make_async_copy(source, low_ref.at[turn], in_sems.at[turn]).start()

    def save(turn):
        start = (turn % per_micro) * span
        return pltpu.make_async_copy(
            wide_ref.at[turn % 2],
            out_hbm.at[order_ref[turn // per_micro], pl.ds(start, span)],
            out_sems.at[turn % 2],
        )

    for turn in range(rounds):
        fetch(turn)
    for turn in range(rounds):
        pltpu.make_async_copy(pieces[0], low_ref.at[turn], in_sems.at[turn]).wait()
        if turn >= 2:
            save(turn - 2).wait()
        wide_ref[turn % 2] = low_ref[turn].astype(jnp.float32)
        save(turn).start()
    save(rounds - 2).wait()
    save(rounds - 1).wait()


def collect(order, pieces, micros, tokens):
    span, width = pieces[0].shape
    rounds = micros * tokens // span
    return pl.pallas_call(
        collect_kernel,
        in_specs=[SM] + [HB_SPEC] * len(pieces),
        out_specs=HB_SPEC,
        out_shape=pltpu.HBM((micros, tokens, width), jnp.float32),
        scratch_shapes=[
            pltpu.VMEM((rounds, span, width), jnp.bfloat16),
            pltpu.VMEM((2, span, width), jnp.float32),
            pltpu.SemaphoreType.DMA((rounds,)),
            pltpu.SemaphoreType.DMA((2,)),
        ],
        compiler_params=pltpu.CompilerParams(vmem_limit_bytes=12 * 1024 * 1024),
        name="collect_part",
    )(order, *[in_hbm(part) for part in pieces])


def weight_kernel(
    x_ref, gl_ref, inv_ref, gain_ref, gp_ref, act_ref, ga_ref, out_hbm, left_ref, right_ref, part_ref, sems
):
    shards = out_hbm.shape[0]
    rows = act_ref.shape[1]
    inv = inv_ref[:, 0:1]
    dims = (((0,), (0,)), ((), ()))
    tokens = x_ref.shape[0]
    slots = part_ref.shape[0]
    right_ref[0:tokens, :] = gp_ref[...]
    right_ref[tokens:, :] = act_ref[...]

    def save(i, slot):
        return pltpu.make_async_copy(part_ref.at[slot], out_hbm.at[i ^ 1], sems.at[slot])

    def step(turn, carry):
        for slot in range(slots):
            i = turn * slots + slot

            @pl.when(turn > 0)
            def _():
                save(i - slots, slot).wait()

            cols = pl.ds(pl.multiple_of(i * rows, rows), rows)
            normed = x_ref[:, cols].astype(jnp.float32) * inv
            hidden = (normed * gain_ref[:, cols]).astype(jnp.bfloat16)
            left_ref[slot, 0:tokens, :] = hidden
            left_ref[slot, tokens:, :] = gl_ref[:, cols]
            total = lax.dot_general(
                left_ref[slot], right_ref[...], dims, preferred_element_type=jnp.float32
            )
            part_ref[slot, 0:rows, :] = total.astype(jnp.bfloat16)
            gain_sum = jnp.sum(ga_ref[:, cols], axis=0, keepdims=True)
            part_ref[slot, rows : rows + PAD, :] = jnp.broadcast_to(gain_sum, (PAD, rows)).astype(
                jnp.bfloat16
            )
            save(i, slot).start()
        return carry

    lax.fori_loop(0, shards // slots, step, 0)
    for slot in range(slots):
        save(shards - slots + slot, slot).wait()


def weight_partial(inputs, grad_low, inv, gain, grad_pre, act, gain_terms):
    adapter = act.shape[1]
    shards = inputs.shape[1] // adapter
    return pl.pallas_call(
        weight_kernel,
        in_specs=[VM] * 7,
        out_specs=HB_SPEC,
        out_shape=pltpu.HBM((shards, adapter + PAD, adapter), jnp.bfloat16),
        scratch_shapes=[
            pltpu.VMEM((4, 2 * inputs.shape[0], adapter), jnp.bfloat16),
            pltpu.VMEM((2 * inputs.shape[0], adapter), jnp.bfloat16),
            pltpu.VMEM((4, adapter + PAD, adapter), jnp.bfloat16),
            pltpu.SemaphoreType.DMA((4,)),
        ],
        compiler_params=pltpu.CompilerParams(vmem_limit_bytes=12 * 1024 * 1024),
        name="weight_part",
    )(*[in_vmem(part) for part in (inputs, grad_low, inv, gain, grad_pre, act, gain_terms)])


def per_device(
    section_inputs, top_grads, weights, norm_gains, feedback, rotation_bits, batch_order
):
    f32, bf16 = jnp.float32, jnp.bfloat16
    micros, tokens, width = section_inputs.shape[1:]
    adapter = weights.shape[2]
    core = lax.axis_index("core")
    keep = lax.axis_index("zl") != core
    section = 2 * lax.axis_index("y") + 1 - core
    swap, hop = swap_pairs(), hop_pairs()

    def swapped(value):
        return permuted(value, swap)

    gain_row = norm_gains[0]
    gain_hi = gain_row.astype(bf16)
    gain_mid = (gain_row - gain_hi.astype(f32)).astype(bf16)
    gain_lo = (gain_row - gain_hi.astype(f32) - gain_mid.astype(f32)).astype(bf16)
    shard = jnp.concatenate(
        [
            weights[0],
            jnp.stack([gain_hi, gain_mid, gain_lo]),
            jnp.zeros((PAD - 3, adapter), bf16),
        ],
        axis=0,
    )
    shard = jnp.where(keep, shard, swapped(shard))
    gathered = lax.all_gather(shard, GROUP, axis=0)
    weight, weight_t, gain = load(gathered)

    span = C * STREAMS
    rounds = micros * tokens // span
    per_micro = tokens // span
    own, got, fb_own, fb_got = [], [], [], []
    for piece in range(rounds):
        micro = batch_order[piece // per_micro]
        start = (piece % per_micro) * span
        part = lax.dynamic_slice(section_inputs[0], (micro, start, 0), (1, span, width))[0]
        own.append(part)
        if piece < per_micro:
            fb_own.append(feedback[0, start : start + span])
        if piece >= 1:
            part, _ = lax.optimization_barrier((part, gathered[0, 0, 0]))
        got.append(swapped(part))
        if piece < per_micro:
            part = fb_own[piece].astype(bf16)
            if piece >= 1:
                part, _ = lax.optimization_barrier((part, gathered[0, 0, 0]))
            fb_got.append(swapped(part))
    top = jnp.where(batch_order[0] == 0, top_grads, top_grads[::-1])
    top = permuted(top.reshape(micros * tokens, width), top_pairs())
    sign = (1 - 2 * lax.dynamic_index_in_dim(rotation_bits, section, 0)).astype(f32)
    matrix = hadamard(HB)
    chunks = rounds * STREAMS

    def blank(rows, cols, dtype):
        return jax.ShapeDtypeStruct((rows, cols), dtype)

    rows = micros * tokens
    fresh = [
        blank(rows, width, bf16),
        blank(rows, adapter, bf16),
        blank(rows, adapter, f32),
        blank(rows, 128, f32),
        blank(tokens, width, f32),
        blank(rows, adapter, bf16),
        blank(rows, width, bf16),
        blank(chunks * 8, width, f32),
    ] + [blank(C, width, bf16)] * STREAMS
    fixed = (weight, weight_t, gain, sign, matrix)
    ticks = rounds + 7
    pieces, pieces_got = [], []
    for tick in range(ticks):
        if tick < rounds:
            last = min(tick, per_micro - 1)
            ready = prepare(
                tick, weight, own[tick], got[tick], fb_own[last], fb_got[last], gain,
                () if tick == 0 else (inputs, act, slope, inv, carried),
                fresh if tick == 0 else (),
            )
            inputs, act, slope, inv, carried = ready[:5]
            if tick == 0:
                grad_pre, grad_low, gain_terms = ready[5:8]
                arrived = list(ready[8:])
        piece = None
        if tick >= 3:
            arrived[0], pieces_got[tick - 3] = lax.optimization_barrier(
                (arrived[0], pieces_got[tick - 3])
            )
        for stream in range(STREAMS):
            state = (inputs, slope, inv, carried, grad_pre, grad_low, gain_terms)
            sent, state, piece = stage(
                tick, stream, rounds, top, fixed, arrived[stream], state, piece
            )
            inputs, slope, inv, carried, grad_pre, grad_low, gain_terms = state
            if tick < ticks - 1:
                arrived[stream] = permuted(sent, hop)
            if stream == 0 and tick > 0:
                late, _ = lax.optimization_barrier((pieces[-1], sent))
                pieces_got.append(swapped(late))
        pieces.append(piece)
    pieces_got.append(swapped(piece))
    pieces_got[-2], gain_terms = lax.optimization_barrier((pieces_got[-2], gain_terms))
    partial = weight_partial(inputs, grad_low, inv, gain, grad_pre, act, gain_terms)
    share = lax.psum_scatter(
        partial.reshape(-1, adapter), GROUP, scatter_dimension=0, tiled=True
    )
    grads = collect(batch_order, pieces + pieces_got, micros, tokens)
    carried = jnp.where(keep, carried, swapped(carried.astype(bf16)).astype(f32))
    share = jnp.where(keep, share, swapped(share)).astype(f32)
    return (grads[None], share[None, :adapter], share[None, adapter], carried[None])


def solution(mesh):
    fine = Mesh(mesh.devices.reshape(SIZES), AXES)
    return jax.shard_map(
        per_device,
        mesh=fine,
        in_specs=(
            P(SECTION, None, FSDP, None),
            P(None, FSDP, None),
            P(SECTION, FSDP, None),
            P(SECTION, FSDP),
            P(SECTION, FSDP, None),
            P(),
            P(),
        ),
        out_specs=(
            P(SECTION, None, FSDP, None),
            P(SECTION, FSDP, None),
            P(SECTION, FSDP),
            P(SECTION, FSDP, None),
        ),
        check_vma=False,
    )
```
